32 devices in a mesh: gx: 16 (over z, x, core), gy: 2 (over y).
Axes of the slice: x: 2, y: 2, z: 4, core: 2. Of those that a mesh axis runs over, the one named last changes fastest.
Arguments:
- populations: float32 [19, 16, 256, 256], P(None, None, 'gx', 'gy'), as said below
- solid_mask: int32 [16, 256, 256], P(None, 'gx', 'gy'), may hold values 0 or 1
- bead_states: float32 [16, 2, 8, 9, 1280], P('gx', 'gy'), as said below
- bead_bricks: int32 [16, 2, 8, 20], P('gx', 'gy'), may hold values from 0 to 63, as said below
- leave_dir: int32 [16, 2, 8], P('gx', 'gy'), may hold values from 0 to 4, as said below
- stiffness: bfloat16 [1280, 1280], replicated, may hold values from -0.15625 to 0.15625
Outputs:
- populations_out: float32 [19, 16, 256, 256], P(None, None, 'gx', 'gy')
- vertex_out: float32 [16, 2, 16, 9, 1280], P('gx', 'gy')
The draws below stay inside these ranges and needn't reach their ends.
Inputs may be any that keep to these rules, and one draw needn't show every extreme that they name: `populations`: every entry is positive. `bead_states`: in the second dimension from the end, entries 0 to 2 are a vertex's x, y, z cell coordinates inside its block's brick, from 1 to 6; entries 3 to 5 its displacement from the reference shape; entries 6 to 8 its velocity. Every slot holds a bead. `bead_bricks`: a brick index counted in the tile that holds the bead after migration. `leave_dir`: 0 keeps the bead on its tile; 1 and 2 move it to the next tile along +x and -x, 3 and 4 along +y and -y. On every tile at most 2 beads have any one code from 1 to 4, and exactly 2 have one of them.
All inputs are finite; a program needn't handle non-finite values. No bound on the sum of `solid_mask` on one device may be relied on, other than what follows from the above.
Results may differ from the reference program's by a relative error of at most 0.00036.
Values sent between devices are 32-bit elements; how exact they have to be, the bound alone decides.
A program may use at most 128 MiB of HBM per device.

```python
from functools import partial
import jax
import jax.numpy as jnp
import numpy as np
from jax import lax

VERTICES = 1280
BLOCKS = 20
NZ = 16
CX = 16
CY = 128
SLOTS = 8
MIG = 2
ALL_SLOTS = 16
BRICKS = 64
NX = 256
NY = 256
N_GX = 16
N_GY = 2


WEIGHTS = np.array([1.0 / 3.0] + [1.0 / 18.0] * 6 + [1.0 / 36.0] * 12)


def draw_populations(key, part):
    weights = jnp.asarray(WEIGHTS, jnp.float32).reshape(19, 1, 1, 1)
    shape = (19, NZ, NX, NY)
    noise = jnp.clip(jax.random.normal(key, shape, jnp.float32), -3.0, 3.0)
    return weights * (1.0 + 0.3 * noise)


def draw_bead_states(key, part):
    shape = (N_GX, N_GY, SLOTS, 3, VERTICES)
    first_key, second_key, third_key = jax.random.split(key, 3)
    offsets = jax.random.uniform(first_key, shape, jnp.float32, 1.0, 6.0)
    displacement = 0.3 * jnp.clip(jax.random.normal(second_key, shape, jnp.float32), -4.0, 4.0)
    velocity = 0.05 * jnp.clip(jax.random.normal(third_key, shape, jnp.float32), -4.0, 4.0)
    return jnp.concatenate([offsets, displacement, velocity], axis=3)


def draw_bead_bricks(key, part):
    drawn = jax.random.randint(key, (N_GX, N_GY, SLOTS, BLOCKS), 0, BRICKS, dtype=jnp.int32)
    drawn = drawn.at[0, 0, 0, 0].set(BRICKS - 1)
    drawn = drawn.at[0, 0, 0, BLOCKS - 1].set(0)
    return drawn.astype(jnp.int32)


def draw_leave_dir(key, part):
    tile_count = N_GX * N_GY
    key_list = jax.random.split(key, tile_count)

    def one_tile(tile_key, tile_number):
        perm_key, count_key = jax.random.split(tile_key)
        slot_counts = jax.random.randint(count_key, (4,), 0, MIG, dtype=jnp.int32)
        full_code = tile_number % 4
        slot_counts = jnp.where(jnp.arange(4) == full_code, MIG, slot_counts)
        limits = jnp.cumsum(slot_counts)
        positions = jnp.arange(SLOTS)
        direction_codes = 1 + jnp.sum((positions[:, None] >= limits[None, :]).astype(jnp.int32), axis=1)
        direction_codes = jnp.where(direction_codes == 5, 0, direction_codes).astype(jnp.int32)
        ordering = jax.random.permutation(perm_key, SLOTS)
        return jnp.zeros((SLOTS,), jnp.int32).at[ordering].set(direction_codes)
    result = jax.vmap(one_tile)(key_list, jnp.arange(tile_count, dtype=jnp.int32))
    return result.reshape(N_GX, N_GY, SLOTS).astype(jnp.int32)


def place_ends(values, own_key, smallest, largest):
    place = [jax.random.randint(jax.random.fold_in(own_key, axis), (), 0, length) for axis, length in enumerate(values.shape)]
    longest = values.shape.index(max(values.shape))
    neighbour = place[:longest] + [(place[longest] + 1) % values.shape[longest]] + place[longest + 1:]
    return values.at[tuple(place)].set(smallest).at[tuple(neighbour)].set(largest)


def gaussian(rng, shape, scale, most, kind=jnp.bfloat16):
    entries = scale * jax.random.normal(rng, shape, jnp.float32)
    return jnp.clip(entries, min=-most, max=most).astype(kind)


def setup_inputs(seed: int = 0) -> dict:
    keys = jax.random.split(jax.random.key(seed), 7)
    populations = draw_populations(jax.random.fold_in(keys[6], 71), 0)
    solid_mask = place_ends((jax.random.randint(keys[1], (NZ, NX, NY), 0, 4) < 1).astype(jnp.int32), jax.random.fold_in(keys[1], 1), 0, 1)
    bead_states = draw_bead_states(jax.random.fold_in(keys[6], 71), 0)
    bead_bricks = draw_bead_bricks(jax.random.fold_in(keys[6], 71), 0)
    leave_dir = draw_leave_dir(jax.random.fold_in(keys[6], 71), 0)
    stiffness = gaussian(keys[5], (VERTICES, VERTICES), VERTICES ** -0.5, 0.15625)
    return {"populations": populations, "solid_mask": solid_mask, "bead_states": bead_states, "bead_bricks": bead_bricks, "leave_dir": leave_dir, "stiffness": stiffness}


LATTICE = np.array([[0, 0, 0], [1, 0, 0], [-1, 0, 0], [0, 1, 0], [0, -1, 0], [0, 0, 1], [0, 0, -1], [1, 1, 0], [-1, -1, 0], [1, -1, 0], [-1, 1, 0], [1, 0, 1], [-1, 0, -1], [1, 0, -1], [-1, 0, 1], [0, 1, 1], [0, -1, -1], [0, 1, -1], [0, -1, 1]])
OPPOSITE = [0, 2, 1, 4, 3, 6, 5, 8, 7, 10, 9, 12, 11, 14, 13, 16, 15, 18, 17]
WEIGHTS = np.array([1.0 / 3.0] + [1.0 / 18.0] * 6 + [1.0 / 36.0] * 12)
RELAX_TIME = 0.8
HIGHEST = lax.Precision.HIGHEST


def kernel_weight(distance):
    inside = jnp.abs(distance) < 2.0
    return jnp.where(inside, 0.25 * (1.0 + jnp.cos(0.5 * jnp.pi * distance)), 0.0 * distance)


def block_weights(block_offsets):
    cell_steps = jnp.arange(8).astype(block_offsets.dtype)
    factors = kernel_weight(block_offsets[:, :, :, None] - cell_steps)
    along_x = factors[:, 0]
    along_y = factors[:, 1]
    along_z = factors[:, 2]
    weight_table = along_z[:, :, :, None, None] * along_x[:, :, None, :, None] * along_y[:, :, None, None, :]
    return weight_table.reshape(block_offsets.shape[0], 64, 512)


def moments(read):
    lattice = jnp.asarray(LATTICE, read.dtype)
    density = jnp.sum(read, axis=0)
    momentum = jnp.tensordot(lattice.T, read, axes=1, precision=HIGHEST)
    return density, momentum


def collide(read, momentum, density, force, solid_mask):
    lattice = jnp.asarray(LATTICE, read.dtype)
    weights = jnp.asarray(WEIGHTS, read.dtype).reshape(19, 1, 1, 1)
    velocity = (momentum + 0.5 * force) / density
    projected = jnp.tensordot(lattice, velocity, axes=1, precision=HIGHEST)
    force_along = jnp.tensordot(lattice, force, axes=1, precision=HIGHEST)
    speed_square = jnp.sum(velocity * velocity, axis=0)
    force_dot = jnp.sum(velocity * force, axis=0)
    equilibrium = weights * density * (1.0 + 3.0 * projected + 4.5 * projected * projected - 1.5 * speed_square)
    source = weights * (3.0 * force_along - 3.0 * force_dot + 9.0 * projected * force_along)
    relaxed = read - (read - equilibrium) / RELAX_TIME + (1.0 - 0.5 / RELAX_TIME) * source
    bounced = jnp.stack([read[lattice_index] for lattice_index in OPPOSITE])
    return jnp.where(solid_mask[None] == 1, bounced, relaxed)


def to_bricks(field):
    depth, width, height = field.shape[1], field.shape[2], field.shape[3]
    blocked = field.reshape(3, depth // 8, 8, width // 8, 8, height // 8, 8)
    blocked = blocked.transpose(1, 3, 5, 0, 2, 4, 6)
    return blocked.reshape(-1, 3, 512)


def from_bricks(blocked, depth, width, height):
    shaped = blocked.reshape(depth // 8, width // 8, height // 8, 3, 8, 8, 8)
    shaped = shaped.transpose(3, 0, 4, 1, 5, 2, 6)
    return shaped.reshape(3, depth, width, height)


def outbox(states, bricks, leaving, code):
    chosen = (leaving == code).astype(jnp.int32)
    ranking = jnp.cumsum(chosen) - 1
    targets = jnp.arange(MIG)
    picker = ((chosen[None, :] == 1) & (ranking[None, :] == targets[:, None])).astype(states.dtype)
    moved = jnp.einsum('ms,scv->mcv', picker, states, precision=HIGHEST)
    moved_bricks = jnp.einsum('ms,sb->mb', picker, bricks.astype(states.dtype), precision=HIGHEST)
    valid = jnp.sum(picker, axis=1)
    return moved, moved_bricks, valid


def couple_tile(velocity_bricks, states, bricks, active, stiffness):
    slot_count = states.shape[0]
    vertices = states.shape[2]
    per_slot = vertices // 64
    displacement = states[:, 3:6, :].astype(jnp.bfloat16)
    product = jnp.dot(displacement.reshape(slot_count * 3, vertices).astype(jnp.float32), stiffness.astype(jnp.float32), precision=HIGHEST)
    node_force = -product.reshape(slot_count, 3, vertices) * active[:, None, None]
    force_sample = node_force.astype(jnp.bfloat16).astype(states.dtype)
    velocity_sample = velocity_bricks.astype(jnp.bfloat16).astype(states.dtype)

    def blockify(values):
        shaped = values.reshape(slot_count, 3, per_slot, 64).transpose(0, 2, 1, 3)
        return shaped.reshape(slot_count * per_slot, 3, 64)

    groups = 8
    block_total = slot_count * per_slot
    group_size = block_total // groups
    positions = blockify(states[:, 0:3, :]).reshape(groups, group_size, 3, 64)
    forces = blockify(force_sample).reshape(groups, group_size, 3, 64)
    brick_list = bricks.reshape(groups, group_size).astype(jnp.int32)

    def couple_group(brick_force, pieces):
        block_offsets, block_force, where_brick = pieces
        weight_table = block_weights(block_offsets).astype(jnp.bfloat16).astype(block_offsets.dtype)
        nearby = velocity_sample[where_brick]
        sampled = jnp.einsum('bcq,bvq->bcv', nearby, weight_table, precision=HIGHEST)
        spread = jnp.einsum('bcv,bvq->bcq', block_force, weight_table, precision=HIGHEST)
        brick_force = brick_force.at[where_brick].add(spread)
        return brick_force, sampled

    start_force = jnp.zeros(velocity_bricks.shape, node_force.dtype)
    brick_force, sampled = lax.scan(couple_group, start_force, (positions, forces, brick_list))
    vertex_velocity = sampled.reshape(slot_count, per_slot, 3, 64).transpose(0, 2, 1, 3).reshape(slot_count, 3, vertices)
    half_step = 0.5 * (states[:, 6:9, :] + vertex_velocity)
    result = jnp.concatenate([states[:, 0:3, :] + half_step, states[:, 3:6, :] + half_step, vertex_velocity], axis=1)
    return brick_force, result * active[:, None, None]


def migrate(bead_states, bead_bricks, leave_dir):
    boxes = []
    for code in range(1, 5):
        boxes.append(jax.vmap(jax.vmap(partial(outbox, code=code)))(bead_states, bead_bricks, leave_dir))
    lower_x = jax.tree.map(partial(jnp.roll, shift=1, axis=0), boxes[0])
    upper_x = jax.tree.map(partial(jnp.roll, shift=-1, axis=0), boxes[1])
    lower_y = jax.tree.map(partial(jnp.roll, shift=1, axis=1), boxes[2])
    upper_y = jax.tree.map(partial(jnp.roll, shift=-1, axis=1), boxes[3])
    keeping = (leave_dir == 0).astype(bead_states.dtype)
    kept_states = bead_states * keeping[..., None, None]
    kept_bricks = bead_bricks.astype(bead_states.dtype) * keeping[..., None]
    received = [lower_x, upper_x, lower_y, upper_y]
    states = jnp.concatenate([kept_states] + [entry[0] for entry in received], axis=2)
    bricks = jnp.concatenate([kept_bricks] + [entry[1] for entry in received], axis=2)
    active = jnp.concatenate([keeping] + [entry[2] for entry in received], axis=2)
    return states, bricks.astype(jnp.int32), active


def reference(populations, solid_mask, bead_states, bead_bricks, leave_dir, stiffness):
    pulled = []
    for lattice_index in range(19):
        shift_x = int(LATTICE[lattice_index, 0])
        shift_y = int(LATTICE[lattice_index, 1])
        shift_z = int(LATTICE[lattice_index, 2])
        pulled.append(jnp.roll(populations[lattice_index], (shift_z, shift_x, shift_y), axis=(0, 1, 2)))
    read = jnp.stack(pulled)
    density, momentum = moments(read)
    fluid_velocity = momentum / density
    states, bricks, active = migrate(bead_states, bead_bricks, leave_dir)
    tile_count = N_GX * N_GY
    tile_velocity = fluid_velocity.reshape(3, NZ, N_GX, CX, N_GY, CY).transpose(2, 4, 0, 1, 3, 5).reshape(tile_count, 3, NZ, CX, CY)

    def per_tile(pieces):
        tile_field, tile_states, tile_bricks, tile_active = pieces
        return couple_tile(to_bricks(tile_field), tile_states, tile_bricks, tile_active, stiffness)

    brick_force, vertex_out = lax.map(per_tile, (tile_velocity, states.reshape(tile_count, ALL_SLOTS, 9, VERTICES), bricks.reshape(tile_count, ALL_SLOTS, BLOCKS), active.reshape(tile_count, ALL_SLOTS)))
    tile_force = jax.vmap(partial(from_bricks, depth=NZ, width=CX, height=CY))(brick_force)
    body_force = tile_force.reshape(N_GX, N_GY, 3, NZ, CX, CY).transpose(2, 3, 0, 4, 1, 5).reshape(3, NZ, NX, NY)
    populations_out = collide(read, momentum, density, body_force, solid_mask)
    return populations_out, vertex_out.reshape(N_GX, N_GY, ALL_SLOTS, 9, VERTICES)
```

```python
import functools

import jax
import jax.numpy as jnp
import numpy as np
from jax import lax
from jax.experimental import pallas as pl
from jax.experimental.pallas import tpu as pltpu
from jax.sharding import PartitionSpec as P

MIG = 2
LATTICE = [
    (0, 0, 0),
    (1, 0, 0), (-1, 0, 0),
    (0, 1, 0), (0, -1, 0),
    (0, 0, 1), (0, 0, -1),
    (1, 1, 0), (-1, -1, 0),
    (1, -1, 0), (-1, 1, 0),
    (1, 0, 1), (-1, 0, -1),
    (1, 0, -1), (-1, 0, 1),
    (0, 1, 1), (0, -1, -1),
    (0, 1, -1), (0, -1, 1),
]
WEIGHTS = [1.0 / 3.0] + [1.0 / 18.0] * 6 + [1.0 / 36.0] * 12
X_UP = [q for q in range(19) if LATTICE[q][0] == 1]
X_DOWN = [q for q in range(19) if LATTICE[q][0] == -1]
Y_UP = [q for q in range(19) if LATTICE[q][1] == 1]
Y_DOWN = [q for q in range(19) if LATTICE[q][1] == -1]
MESH = pl.DeviceIdType.MESH
COS_FIT = [
    float(c)
    for c in np.polynomial.Chebyshev.interpolate(
        lambda u: np.cos(np.pi * np.sqrt(np.maximum(u, 0.0)) / 4.0), 5, domain=[0.0, 4.0]
    ).convert(kind=np.polynomial.Polynomial).coef
]


def exchange_kernel(
    sizes,
    leave_ref,
    states_ref,
    bricks_ref,
    pops_ref,
    beads_ref,
    meta_ref,
    xface_ref,
    yface_ref,
    corner_ref,
    bead_out,
    x_out,
    y_out,
    send_sems,
    recv_sems,
):
    n_gx, n_gy = sizes
    depth, width = pops_ref.shape[1], pops_ref.shape[2]
    slots = states_ref.shape[0]
    tiles = states_ref.shape[2] // 128
    blocks = bricks_ref.shape[1]
    ax, ay = lax.axis_index("gx"), lax.axis_index("gy")
    xp, xm = lax.rem(ax + 1, n_gx), lax.rem(ax + n_gx - 1, n_gx)
    yp, ym = lax.rem(ay + 1, n_gy), lax.rem(ay + n_gy - 1, n_gy)
    barrier = pltpu.get_barrier_semaphore()
    for where in ((xp, ay), (xm, ay), (ax, yp), (ax, ym), (xp, yp), (xm, ym), (xp, ym), (xm, yp)):
        pl.semaphore_signal(barrier, inc=1, device_id=where, device_id_type=MESH)

    for i, q in enumerate(X_UP):
        x_out[0, i] = pops_ref[q, :, width - 1, :]
    for i, q in enumerate(X_DOWN):
        x_out[1, i] = pops_ref[q, :, 0, :]

    leaving = [leave_ref[0, s] for s in range(slots)]
    for d in range(4):
        first, second, count = jnp.int32(0), jnp.int32(0), jnp.int32(0)
        for s in range(slots):
            hit = leaving[s] == d + 1
            first = jnp.where(hit & (count == 0), s, first)
            second = jnp.where(hit & (count == 1), s, second)
            count = count + jnp.where(hit, 1, 0)
        for m, at in enumerate((first, second)):
            for j in range(tiles):
                bead_out[d, (m * tiles + j) * 8 : (m * tiles + j + 1) * 8, :] = states_ref[
                    at, 0:8, j * 128 : (j + 1) * 128
                ]
                row = MIG * tiles * 8 + m * tiles + j
                bead_out[d, row : row + 1, :] = states_ref[at, 8:9, j * 128 : (j + 1) * 128]
            row = MIG * tiles * 9 + m
            valid = jnp.where(count > m, 1.0, 0.0).astype(jnp.float32)
            bead_out[d, row : row + 1, :] = jnp.full((1, 128), valid, jnp.float32)
            bead_out[d, row : row + 1, 0:blocks] = bricks_ref[pl.ds(at, 1), :].astype(jnp.float32)

    pl.semaphore_wait(barrier, 8)
    copies = []

    def send(src, dst, where):
        at = len(copies)
        copy = pltpu.make_async_remote_copy(
            src_ref=src,
            dst_ref=dst,
            send_sem=send_sems.at[at],
            recv_sem=recv_sems.at[at],
            device_id=where,
            device_id_type=MESH,
        )
        copy.start()
        copies.append(copy)

    targets = ((xp, ay), (xm, ay), (ax, yp), (ax, ym))
    for d in (2, 3, 0, 1):
        send(bead_out.at[d], beads_ref.at[d], targets[d])
    send(x_out.at[0], xface_ref.at[0], targets[0])
    send(x_out.at[1], xface_ref.at[1], targets[1])

    lane = lax.broadcasted_iota(jnp.int32, (width, 128), 1)
    for side, (group, edge) in enumerate(((Y_UP, 127), (Y_DOWN, 0))):
        packed = jnp.zeros((width, 128), jnp.float32)
        for i, q in enumerate(group):
            for z in range(depth):
                t = i * depth + z
                packed = jnp.where(
                    lane == t, pltpu.roll(pops_ref[q, z], (t - edge) % 128, 1), packed
                )
        y_out[side] = packed
    send(y_out.at[0], yface_ref.at[0], targets[2])
    send(y_out.at[1], yface_ref.at[1], targets[3])
    send(y_out.at[0, width - 8 : width], corner_ref.at[0], (xp, yp))
    send(y_out.at[1, 0:8], corner_ref.at[1], (xm, ym))
    send(y_out.at[1, width - 8 : width], corner_ref.at[2], (xp, ym))
    send(y_out.at[0, 0:8], corner_ref.at[3], (xm, yp))
    for copy in copies:
        copy.wait()
    row = MIG * tiles * 9
    for d in range(4):
        meta_ref[d * MIG : (d + 1) * MIG, :] = beads_ref[d, row : row + MIG, :].astype(jnp.int32)


def exchange(populations, states, bricks, leaving, sizes):
    depth, width = populations.shape[1], populations.shape[2]
    tiles = states.shape[2] // 128
    rows = -(-MIG * (tiles * 9 + 1) // 8) * 8
    vmem = pl.BlockSpec(memory_space=pltpu.VMEM)
    smem = pl.BlockSpec(memory_space=pltpu.SMEM)
    f32 = jnp.float32
    return pl.pallas_call(
        functools.partial(exchange_kernel, sizes),
        out_shape=(
            jax.ShapeDtypeStruct((4, rows, 128), f32),
            jax.ShapeDtypeStruct((4 * MIG, 128), jnp.int32),
            jax.ShapeDtypeStruct((2, 5, depth, 128), f32),
            jax.ShapeDtypeStruct((2, width, 128), f32),
            jax.ShapeDtypeStruct((4, 8, 128), f32),
        ),
        in_specs=[smem, vmem, vmem, vmem],
        out_specs=(vmem,) * 5,
        scratch_shapes=[
            pltpu.VMEM((4, rows, 128), f32),
            pltpu.VMEM((2, 5, depth, 128), f32),
            pltpu.VMEM((2, width, 128), f32),
            pltpu.SemaphoreType.DMA((12,)),
            pltpu.SemaphoreType.DMA((12,)),
        ],
        compiler_params=pltpu.CompilerParams(
            collective_id=0, has_side_effects=True, vmem_limit_bytes=24 * 1024 * 1024
        ),
        name="exchange",
    )(leaving, states, bricks, populations)


def phi(distance):
    square = distance * distance
    u = jnp.minimum(square, 4.0)
    value = jnp.full_like(u, COS_FIT[5])
    for c in COS_FIT[4::-1]:
        value = value * u + c
    return jnp.where(square < 4.0, 0.5 * value * value, 0.0)


def step_kernel(
    leave_ref,
    bricks_ref,
    meta_ref,
    states_ref,
    beads_ref,
    xface_ref,
    yface_ref,
    corner_ref,
    solid_ref,
    pops_ref,
    stiff_ref,
    pops_out,
    vertex_ref,
    read_ref,
    moment_ref,
    field_ref,
    velocity_ref,
    force_ref,
    moved_ref,
    node_ref,
    diagonal_ref,
    weight_ref,
    slot_ref,
    sems,
):
    depth, width = pops_ref.shape[1], pops_ref.shape[2]
    slots = states_ref.shape[0]
    vertices = states_ref.shape[2]
    tiles = vertices // 128
    quads = vertices // 256
    bx_count, by_count = width // 8, 16
    f32 = jnp.float32

    for s in range(slots):
        moved_ref[s] = states_ref[s]
    for d in range(4):
        for m in range(MIG):
            s = slots + d * MIG + m
            for j in range(tiles):
                at = (m * tiles + j) * 8
                moved_ref[s, 0:8, j * 128 : (j + 1) * 128] = beads_ref[d, at : at + 8, :]
                row = MIG * tiles * 8 + m * tiles + j
                moved_ref[s, 8:9, j * 128 : (j + 1) * 128] = beads_ref[d, row : row + 1, :]
    count = jnp.int32(0)
    blocks = bricks_ref.shape[1]
    for s in range(slots):
        slot_ref[count] = s
        count = count + jnp.where(leave_ref[0, s] == 0, 1, 0)
    for s in range(4 * MIG):
        slot_ref[count] = slots + s
        count = count + jnp.where(meta_ref[s, blocks] > 0, 1, 0)

    total = slots + 4 * MIG
    rows = jnp.concatenate(
        [moved_ref[s, 0:8, :].astype(jnp.bfloat16) for s in range(total)], axis=0
    )
    for g in range(quads):
        part = jnp.dot(
            rows, stiff_ref[:, g * 256 : (g + 1) * 256], preferred_element_type=f32
        )
        node_ref[:, g * 256 : (g + 1) * 256] = -part

    row8 = lax.broadcasted_iota(jnp.int32, (width, 128), 0)
    lane = lax.broadcasted_iota(jnp.int32, (width, 128), 1)
    for i, (side, up) in enumerate(((0, True), (1, False), (1, True), (0, False))):
        face = yface_ref[side]
        if up:
            edge = jnp.broadcast_to(corner_ref[i, 7:8, :], (width, 128))
            diagonal_ref[i] = jnp.where(row8 == 0, edge, pltpu.roll(face, 1, 0))
        else:
            edge = jnp.broadcast_to(corner_ref[i, 0:1, :], (width, 128))
            diagonal_ref[i] = jnp.where(row8 == width - 1, edge, pltpu.roll(face, width - 1, 0))

    def pull(z, carry):
        density = None
        sums = [None, None, None]
        for q in range(19):
            cx, cy, cz = LATTICE[q]
            zs = z if cz == 0 else lax.rem(z - cz + depth, depth)
            value = pops_ref[q, zs]
            if cx == 1:
                edge = xface_ref[0, X_UP.index(q), pl.ds(zs, 1), :]
                value = jnp.where(row8 == 0, edge, pltpu.roll(value, 1, 0))
            elif cx == -1:
                edge = xface_ref[1, X_DOWN.index(q), pl.ds(zs, 1), :]
                value = jnp.where(row8 == width - 1, edge, pltpu.roll(value, width - 1, 0))
            if cy != 0:
                face = diagonal_ref[q - 7] if cx != 0 else yface_ref[0 if cy == 1 else 1]
                t = (Y_UP if cy == 1 else Y_DOWN).index(q) * depth + zs
                if cy == 1:
                    edge = pltpu.roll(face, lax.rem(128 - t, 128), 1)
                    value = jnp.where(lane == 0, edge, pltpu.roll(value, 1, 1))
                else:
                    edge = pltpu.roll(face, 127 - t, 1)
                    value = jnp.where(lane == 127, edge, pltpu.roll(value, 127, 1))
            read_ref[q, z] = value
            density = value if density is None else density + value
            for axis, c in enumerate((cx, cy, cz)):
                if c == 1:
                    sums[axis] = value if sums[axis] is None else sums[axis] + value
                elif c == -1:
                    sums[axis] = sums[axis] - value
        inverse = 1.0 / density
        moment_ref[0, z] = density
        moment_ref[4, z] = inverse
        for axis in range(3):
            moment_ref[1 + axis, z] = sums[axis]
            field_ref[axis, z] = (sums[axis] * inverse).astype(jnp.bfloat16).astype(f32)
        return carry

    lax.fori_loop(0, depth, pull, 0)

    force_ref[...] = jnp.zeros_like(force_ref)
    velocity_ref[...] = jnp.zeros_like(velocity_ref)
    lane8 = lax.broadcasted_iota(jnp.int32, (8, 128), 1)
    for axis in range(3):
        for bz in range(depth // 8):
            cells = jnp.concatenate(
                [
                    field_ref[axis, bz * 8 + iz, bx * 8 : bx * 8 + 8, :]
                    for bx in range(bx_count)
                    for iz in range(8)
                ],
                axis=0,
            )
            turned = cells.T
            for by in range(by_count):
                here = turned[by * 8 : by * 8 + 8, :]
                across = pltpu.roll(here, 64, 1)
                lower = pltpu.roll(here, 4, 0)
                both = pltpu.roll(across, 4, 0)
                for bx, (a, b) in enumerate(((here, both), (across, lower))):
                    brick = (bz * bx_count + bx) * by_count + by
                    laid = jnp.where(lane8 < 64, a, b)
                    for k in range(4):
                        velocity_ref[brick, k, axis : axis + 1, :] = laid[k : k + 1, :]

    for s in range(total):
        vertex_ref[s] = jnp.zeros_like(vertex_ref[s])
    steps8 = lax.broadcasted_iota(jnp.int32, (8, 256), 0).astype(f32)
    group = lax.broadcasted_iota(jnp.int32, (8, 256), 1) // 64

    def couple(i, carry):
        s = slot_ref[i]
        own = s < slots
        inside = jnp.minimum(s, slots - 1)
        outside = jnp.maximum(s - slots, 0)
        start = pl.multiple_of(s * 8, 8)
        for g in range(quads):
            cols = slice(g * 256, (g + 1) * 256)
            where = [
                jnp.where(own, bricks_ref[inside, 4 * g + j], meta_ref[outside, 4 * g + j])
                for j in range(4)
            ]
            state = moved_ref[s, :, cols]
            along_x = phi(state[0:1, :] - steps8)
            along_y = phi(state[1:2, :] - steps8)
            along_z = phi(state[2:3, :] - steps8)
            zx = [along_z[iz : iz + 1, :] * along_x for iz in range(8)]
            for k in range(4):
                for h in range(2):
                    iy = k + 4 * h
                    y_row = jnp.broadcast_to(along_y[iy : iy + 1, :], (8, 256))
                    for iz in range(0, 8, 2):
                        pair = jnp.concatenate([zx[iz] * y_row, zx[iz + 1] * y_row], axis=0)
                        at = (k * 2 + h) * 64 + iz * 8
                        weight_ref[g, at : at + 16, :] = pair.astype(jnp.bfloat16)
            near = jnp.concatenate(
                [
                    jnp.concatenate([velocity_ref[r, k] for k in range(4)], axis=1)
                    for r in where
                ],
                axis=0,
            ).astype(jnp.bfloat16)
            sampled = jnp.dot(near, weight_ref[g], preferred_element_type=f32)
            force = node_ref[pl.ds(start, 8), cols]
            spreading = jnp.concatenate(
                [jnp.where(group == j, force, 0.0) for j in range(4)], axis=0
            ).astype(jnp.bfloat16)
            spread = lax.dot_general(
                spreading, weight_ref[g], (((1,), (1,)), ((), ())), preferred_element_type=f32
            )
            for j in range(4):
                for k in range(4):
                    force_ref[where[j], k] = (
                        force_ref[where[j], k]
                        + spread[8 * j : 8 * j + 8, k * 128 : (k + 1) * 128]
                    )
            vertex = jnp.zeros((8, 256), f32)
            for j in range(4):
                vertex = jnp.where(group == j, sampled[8 * j : 8 * j + 8, :], vertex)
            vertex = vertex[0:3, :]
            half = 0.5 * (state[6:9, :] + vertex)
            vertex_ref[s, :, cols] = jnp.concatenate(
                [state[0:3, :] + half, state[3:6, :] + half, vertex], axis=0
            )
        return carry

    lax.fori_loop(0, count, couple, 0)

    for axis in range(3):
        for bz in range(depth // 8):
            parts = []
            for by in range(by_count):
                laid = []
                for bx in range(bx_count):
                    brick = (bz * bx_count + bx) * by_count + by
                    got = [force_ref[brick, k, 3 + axis : 4 + axis, :] for k in range(4)]
                    laid.append(jnp.concatenate(got + got, axis=0))
                top = lax.broadcasted_iota(jnp.int32, (8, 128), 0) < 4
                low = jnp.where(top, laid[0], pltpu.roll(laid[0], 64, 1))
                high = jnp.where(top, pltpu.roll(laid[1], 64, 1), laid[1])
                parts.append(jnp.where(lane8 < 64, low, high))
            cells = jnp.concatenate(parts, axis=0).T
            for bx in range(bx_count):
                for iz in range(8):
                    at = (bx * 8 + iz) * 8
                    field_ref[axis, bz * 8 + iz, bx * 8 : bx * 8 + 8, :] = cells[at : at + 8, :]

    def collide(z, carry):
        density, inverse = moment_ref[0, z], moment_ref[4, z]
        force = [field_ref[axis, z] for axis in range(3)]
        speed = [(moment_ref[1 + axis, z] + 0.5 * force[axis]) * inverse for axis in range(3)]
        square = speed[0] * speed[0] + speed[1] * speed[1] + speed[2] * speed[2]
        dot = speed[0] * force[0] + speed[1] * force[1] + speed[2] * force[2]
        fluid = solid_ref[z] == 0
        base = (1.25 * density) * (1.0 - 1.5 * square) - 1.125 * dot
        dense = 5.625 * density
        odd = [3.75 * density * speed[axis] + 1.125 * force[axis] for axis in range(3)]
        slope = [3.375 * force[axis] for axis in range(3)]
        rest = read_ref[0, z]
        read_ref[0, z] = jnp.where(fluid, WEIGHTS[0] * base - 0.25 * rest, rest)

        def along(vector, c):
            terms = None
            for axis in range(3):
                if c[axis] == 0:
                    continue
                if terms is None:
                    terms = vector[axis] if c[axis] == 1 else -vector[axis]
                else:
                    terms = terms + vector[axis] if c[axis] == 1 else terms - vector[axis]
            return terms

        for q in range(1, 19, 2):
            c = LATTICE[q]
            e = along(speed, c)
            even = WEIGHTS[q] * (base + e * (dense * e + along(slope, c)))
            skew = WEIGHTS[q] * along(odd, c)
            ahead, back = read_ref[q, z], read_ref[q + 1, z]
            read_ref[q, z] = jnp.where(fluid, even + skew - 0.25 * ahead, back)
            read_ref[q + 1, z] = jnp.where(fluid, even - skew - 0.25 * back, ahead)
        pltpu.make_async_copy(read_ref.at[:, z], pops_out.at[:, z], sems.at[z]).start()
        return carry

    lax.fori_loop(0, depth, collide, 0)

    def finish(z, carry):
        pltpu.make_async_copy(read_ref.at[:, z], pops_out.at[:, z], sems.at[z]).wait()
        return carry

    lax.fori_loop(0, depth, finish, 0)


def advance(leaving, bricks, meta, states, beads, xface, yface, corner, solid, pops, stiffness):
    depth, width = pops.shape[1], pops.shape[2]
    slots, vertices = states.shape[0], states.shape[2]
    total = slots + 4 * MIG
    n_bricks = (depth // 8) * (width // 8) * 16
    vmem = pl.BlockSpec(memory_space=pltpu.VMEM)
    smem = pl.BlockSpec(memory_space=pltpu.SMEM)
    f32 = jnp.float32
    return pl.pallas_call(
        step_kernel,
        out_shape=(
            jax.ShapeDtypeStruct(pops.shape, f32),
            jax.ShapeDtypeStruct((total, 9, vertices), f32),
        ),
        in_specs=[smem, smem, smem] + [vmem] * 8,
        out_specs=(pl.BlockSpec(memory_space=pl.ANY), vmem),
        scratch_shapes=[
            pltpu.VMEM(pops.shape, f32),
            pltpu.VMEM((5, depth, width, 128), f32),
            pltpu.VMEM((3, depth, width, 128), f32),
            pltpu.VMEM((n_bricks, 4, 8, 128), f32),
            pltpu.VMEM((n_bricks, 4, 8, 128), f32),
            pltpu.VMEM((total, 9, vertices), f32),
            pltpu.VMEM((total * 8, vertices), f32),
            pltpu.VMEM((4, width, 128), f32),
            pltpu.VMEM((vertices // 256, 512, 256), jnp.bfloat16),
            pltpu.SMEM((total + 1,), jnp.int32),
            pltpu.SemaphoreType.DMA((depth,)),
        ],
        compiler_params=pltpu.CompilerParams(vmem_limit_bytes=48 * 1024 * 1024),
        name="step",
    )(leaving, bricks, meta, states, beads, xface, yface, corner, solid, pops, stiffness)


def solution(mesh):
    sizes = (mesh.shape["gx"], mesh.shape["gy"])

    def local(populations, solid_mask, bead_states, bead_bricks, leave_dir, stiffness):
        states = bead_states.reshape(bead_states.shape[2:])
        bricks = bead_bricks.reshape(bead_bricks.shape[2:])
        leaving = leave_dir.reshape((1,) + leave_dir.shape[2:])
        beads, meta, xface, yface, corner = exchange(populations, states, bricks, leaving, sizes)
        populations_out, vertex_out = advance(
            leaving, bricks, meta, states, beads, xface, yface, corner,
            solid_mask, populations, stiffness,
        )
        return (populations_out, vertex_out.reshape((1, 1) + vertex_out.shape))

    return jax.shard_map(
        local,
        mesh=mesh,
        in_specs=(
            P(None, None, "gx", "gy"),
            P(None, "gx", "gy"),
            P("gx", "gy", None, None, None),
            P("gx", "gy", None, None),
            P("gx", "gy", None),
            P(),
        ),
        out_specs=(P(None, None, "gx", "gy"), P("gx", "gy", None, None, None)),
        check_vma=False,
    )
```

```python
import functools

import jax
import jax.numpy as jnp
import numpy as np
from jax import lax
from jax.experimental import pallas as pl
from jax.experimental.pallas import tpu as pltpu
from jax.sharding import PartitionSpec as P

MIG = 2
LATTICE = [
    (0, 0, 0),
    (1, 0, 0), (-1, 0, 0),
    (0, 1, 0), (0, -1, 0),
    (0, 0, 1), (0, 0, -1),
    (1, 1, 0), (-1, -1, 0),
    (1, -1, 0), (-1, 1, 0),
    (1, 0, 1), (-1, 0, -1),
    (1, 0, -1), (-1, 0, 1),
    (0, 1, 1), (0, -1, -1),
    (0, 1, -1), (0, -1, 1),
]
WEIGHTS = [1.0 / 3.0] + [1.0 / 18.0] * 6 + [1.0 / 36.0] * 12
X_UP = [q for q in range(19) if LATTICE[q][0] == 1]
X_DOWN = [q for q in range(19) if LATTICE[q][0] == -1]
Y_UP = [q for q in range(19) if LATTICE[q][1] == 1]
Y_DOWN = [q for q in range(19) if LATTICE[q][1] == -1]
MESH = pl.DeviceIdType.MESH
COS_FIT = [
    float(c)
    for c in np.polynomial.Chebyshev.interpolate(
        lambda u: np.cos(np.pi * np.sqrt(np.maximum(u, 0.0)) / 4.0), 5, domain=[0.0, 4.0]
    ).convert(kind=np.polynomial.Polynomial).coef
]


def exchange_kernel(
    sizes,
    leave_hbm,
    bricks_hbm,
    states_hbm,
    pops_hbm,
    beads_ref,
    read_hbm,
    moment_hbm,
    velocity_hbm,
    read_ref,
    moment_ref,
    velocity_ref,
    leave_ref,
    bricks_ref,
    states_ref,
    pops_ref,
    bead_out,
    x_out,
    y_out,
    xface_ref,
    yface_ref,
    corner_ref,
    diagonal_ref,
    field_ref,
    load_sems,
    store_sems,
    send_sems,
    recv_sems,
):
    n_gx, n_gy = sizes
    f32 = jnp.float32
    loads = [
        pltpu.make_async_copy(src, dst, load_sems.at[i])
        for i, (src, dst) in enumerate(
            (
                (leave_hbm, leave_ref),
                (bricks_hbm, bricks_ref),
                (states_hbm, states_ref),
                (pops_hbm, pops_ref),
            )
        )
    ]
    for load in loads:
        load.start()
    depth, width = pops_ref.shape[1], pops_ref.shape[2]
    slots = states_ref.shape[1]
    tiles = states_ref.shape[2] // 128
    blocks = bricks_ref.shape[1]
    bx_count, by_count = width // 8, 16
    ax, ay = lax.axis_index("gx"), lax.axis_index("gy")
    xp, xm = lax.rem(ax + 1, n_gx), lax.rem(ax + n_gx - 1, n_gx)
    yp, ym = lax.rem(ay + 1, n_gy), lax.rem(ay + n_gy - 1, n_gy)
    barrier = pltpu.get_barrier_semaphore()
    for where in ((xp, ay), (xm, ay), (ax, yp), (ax, ym), (xp, yp), (xm, ym), (xp, ym), (xm, yp)):
        pl.semaphore_signal(barrier, inc=1, device_id=where, device_id_type=MESH)

    for load in loads[:3]:
        load.wait()
    leaving = [leave_ref[0, s] for s in range(slots)]
    last = MIG * tiles * 8
    row = MIG * tiles * 9
    for d in (2, 3, 0, 1):
        first, second, count = jnp.int32(0), jnp.int32(0), jnp.int32(0)
        for s in range(slots):
            hit = leaving[s] == d + 1
            first = jnp.where(hit & (count == 0), s, first)
            second = jnp.where(hit & (count == 1), s, second)
            count = count + jnp.where(hit, 1, 0)
        for m, at in enumerate((first, second)):
            for c in range(9):
                line = states_ref[c, pl.ds(at, 1), :]
                for j in range(tiles):
                    to = j * 16 + 2 * c + m if c < 8 else last + 2 * j + m
                    bead_out[d, to : to + 1, :] = line[:, j * 128 : (j + 1) * 128]
            valid = jnp.where(count > m, 1.0, 0.0).astype(f32)
            bead_out[d, row + m : row + m + 1, :] = jnp.full((1, 128), valid, f32)
            bead_out[d, row + m : row + m + 1, 0:blocks] = bricks_ref[pl.ds(at, 1), :].astype(f32)

    loads[3].wait()
    for i, q in enumerate(X_UP):
        x_out[0, i] = pops_ref[q, :, width - 1, :]
    for i, q in enumerate(X_DOWN):
        x_out[1, i] = pops_ref[q, :, 0, :]
    lane = lax.broadcasted_iota(jnp.int32, (width, 128), 1)
    for side, (group, edge) in enumerate(((Y_UP, 127), (Y_DOWN, 0))):
        packed = jnp.zeros((width, 128), f32)
        for i, q in enumerate(group):
            for z in range(depth):
                t = i * depth + z
                packed = jnp.where(
                    lane == t, pltpu.roll(pops_ref[q, z], (t - edge) % 128, 1), packed
                )
        y_out[side] = packed

    pl.semaphore_wait(barrier, 8)
    copies = []

    def send(src, dst, where):
        at = len(copies)
        copy = pltpu.make_async_remote_copy(
            src_ref=src,
            dst_ref=dst,
            send_sem=send_sems.at[at],
            recv_sem=recv_sems.at[at],
            device_id=where,
            device_id_type=MESH,
        )
        copy.start()
        copies.append(copy)

    targets = ((xp, ay), (xm, ay), (ax, yp), (ax, ym))
    send(y_out.at[0], yface_ref.at[0], targets[2])
    send(y_out.at[1], yface_ref.at[1], targets[3])
    send(y_out.at[0, width - 8 : width], corner_ref.at[0], (xp, yp))
    send(y_out.at[1, 0:8], corner_ref.at[1], (xm, ym))
    send(y_out.at[1, width - 8 : width], corner_ref.at[2], (xp, ym))
    send(y_out.at[0, 0:8], corner_ref.at[3], (xm, yp))
    send(x_out.at[0], xface_ref.at[0], targets[0])
    send(x_out.at[1], xface_ref.at[1], targets[1])
    for d in (2, 3, 0, 1):
        send(bead_out.at[d], beads_ref.at[d], targets[d])
    for copy in copies[:8]:
        copy.wait_recv()

    row8 = lax.broadcasted_iota(jnp.int32, (width, 128), 0)
    for i, (side, up) in enumerate(((0, True), (1, False), (1, True), (0, False))):
        face = yface_ref[side]
        if up:
            edge = jnp.broadcast_to(corner_ref[i, 7:8, :], (width, 128))
            diagonal_ref[i] = jnp.where(row8 == 0, edge, pltpu.roll(face, 1, 0))
        else:
            edge = jnp.broadcast_to(corner_ref[i, 0:1, :], (width, 128))
            diagonal_ref[i] = jnp.where(row8 == width - 1, edge, pltpu.roll(face, width - 1, 0))

    def pull(z, carry):
        density = None
        sums = [None, None, None]
        for q in range(19):
            cx, cy, cz = LATTICE[q]
            zs = z if cz == 0 else lax.rem(z - cz + depth, depth)
            value = pops_ref[q, zs]
            if cx == 1:
                edge = xface_ref[0, X_UP.index(q), pl.ds(zs, 1), :]
                value = jnp.where(row8 == 0, edge, pltpu.roll(value, 1, 0))
            elif cx == -1:
                edge = xface_ref[1, X_DOWN.index(q), pl.ds(zs, 1), :]
                value = jnp.where(row8 == width - 1, edge, pltpu.roll(value, width - 1, 0))
            if cy != 0:
                face = diagonal_ref[q - 7] if cx != 0 else yface_ref[0 if cy == 1 else 1]
                t = (Y_UP if cy == 1 else Y_DOWN).index(q) * depth + zs
                if cy == 1:
                    edge = pltpu.roll(face, lax.rem(128 - t, 128), 1)
                    value = jnp.where(lane == 0, edge, pltpu.roll(value, 1, 1))
                else:
                    edge = pltpu.roll(face, 127 - t, 1)
                    value = jnp.where(lane == 127, edge, pltpu.roll(value, 127, 1))
            read_ref[q, z] = value
            density = value if density is None else density + value
            for axis, c in enumerate((cx, cy, cz)):
                if c == 1:
                    sums[axis] = value if sums[axis] is None else sums[axis] + value
                elif c == -1:
                    sums[axis] = sums[axis] - value
        inverse = 1.0 / density
        moment_ref[0, z] = density
        moment_ref[4, z] = inverse
        for axis in range(3):
            moment_ref[1 + axis, z] = sums[axis]
            field_ref[axis, z] = (sums[axis] * inverse).astype(jnp.bfloat16).astype(f32)
        pltpu.make_async_copy(read_ref.at[:, z], read_hbm.at[:, z], store_sems.at[z]).start()
        return carry

    lax.fori_loop(0, depth, pull, 0)
    stored = pltpu.make_async_copy(moment_ref, moment_hbm, store_sems.at[depth])
    stored.start()

    velocity_ref[...] = jnp.zeros_like(velocity_ref)
    lane8 = lax.broadcasted_iota(jnp.int32, (8, 128), 1)
    for axis in range(3):
        for bz in range(depth // 8):
            cells = jnp.concatenate(
                [
                    field_ref[axis, bz * 8 + iz, bx * 8 : bx * 8 + 8, :]
                    for bx in range(bx_count)
                    for iz in range(8)
                ],
                axis=0,
            )
            turned = cells.T
            for by in range(by_count):
                here = turned[by * 8 : by * 8 + 8, :]
                across = pltpu.roll(here, 64, 1)
                lower = pltpu.roll(here, 4, 0)
                both = pltpu.roll(across, 4, 0)
                for bx, (a, b) in enumerate(((here, both), (across, lower))):
                    brick = (bz * bx_count + bx) * by_count + by
                    laid = jnp.where(lane8 < 64, a, b)
                    for k in range(4):
                        velocity_ref[brick, k, axis : axis + 1, :] = laid[k : k + 1, :]

    laid_out = pltpu.make_async_copy(velocity_ref, velocity_hbm, store_sems.at[depth + 1])
    laid_out.start()

    def finish(z, carry):
        pltpu.make_async_copy(read_ref.at[:, z], read_hbm.at[:, z], store_sems.at[z]).wait()
        return carry

    lax.fori_loop(0, depth, finish, 0)
    stored.wait()
    for copy in copies[:8]:
        copy.wait_send()
    for copy in copies[8:]:
        copy.wait()
    laid_out.wait()


def exchange(populations, states, bricks, leaving, sizes):
    depth, width = populations.shape[1], populations.shape[2]
    tiles = states.shape[2] // 128
    rows = -(-MIG * (tiles * 9 + 1) // 8) * 8
    n_bricks = (depth // 8) * (width // 8) * 16
    hbm = pl.BlockSpec(memory_space=pltpu.HBM)
    f32 = jnp.float32
    return pl.pallas_call(
        functools.partial(exchange_kernel, sizes),
        out_shape=(
            jax.ShapeDtypeStruct((4, rows, 128), f32),
            jax.ShapeDtypeStruct(populations.shape, f32),
            jax.ShapeDtypeStruct((5, depth, width, 128), f32),
            jax.ShapeDtypeStruct((n_bricks, 4, 8, 128), f32),
        ),
        in_specs=[hbm] * 4,
        out_specs=(hbm,) * 4,
        scratch_shapes=[
            pltpu.VMEM(populations.shape, f32),
            pltpu.VMEM((5, depth, width, 128), f32),
            pltpu.VMEM((n_bricks, 4, 8, 128), f32),
            pltpu.SMEM(leaving.shape, jnp.int32),
            pltpu.VMEM(bricks.shape, jnp.int32),
            pltpu.VMEM(states.shape, f32),
            pltpu.VMEM(populations.shape, f32),
            pltpu.VMEM((4, rows, 128), f32),
            pltpu.VMEM((2, 5, depth, 128), f32),
            pltpu.VMEM((2, width, 128), f32),
            pltpu.VMEM((2, 5, depth, 128), f32),
            pltpu.VMEM((2, width, 128), f32),
            pltpu.VMEM((4, 8, 128), f32),
            pltpu.VMEM((4, width, 128), f32),
            pltpu.VMEM((3, depth, width, 128), f32),
            pltpu.SemaphoreType.DMA((4,)),
            pltpu.SemaphoreType.DMA((depth + 2,)),
            pltpu.SemaphoreType.DMA((12,)),
            pltpu.SemaphoreType.DMA((12,)),
        ],
        compiler_params=pltpu.CompilerParams(
            collective_id=0, has_side_effects=True, vmem_limit_bytes=56 * 1024 * 1024
        ),
        name="exchange",
    )(leaving, bricks, states, populations)


def phi(distance):
    square = distance * distance
    u = jnp.minimum(square, 4.0)
    value = jnp.full_like(u, COS_FIT[5])
    for c in COS_FIT[4::-1]:
        value = value * u + c
    return jnp.where(square < 4.0, 0.5 * value * value, 0.0)


def step_kernel(
    leave_hbm,
    bricks_hbm,
    states_hbm,
    beads_hbm,
    solid_hbm,
    read_hbm,
    moment_hbm,
    velocity_hbm,
    stiff_hbm,
    pops_out,
    vertex_out,
    leave_ref,
    bricks_ref,
    meta_ref,
    states_ref,
    beads_ref,
    solid_ref,
    read_ref,
    moment_ref,
    velocity_ref,
    stiff_ref,
    fresh_ref,
    field_ref,
    force_ref,
    moved_ref,
    node_ref,
    sampled_ref,
    vertex_ref,
    weight_ref,
    slot_ref,
    sems,
    load_sems,
):
    meta_at = beads_hbm.shape[1] - 8
    pairs = [(leave_hbm, leave_ref), (bricks_hbm, bricks_ref)]
    pairs += [(beads_hbm.at[d, meta_at : meta_at + 8], meta_ref.at[d]) for d in range(4)]
    pairs += [(states_hbm, states_ref), (beads_hbm, beads_ref), (stiff_hbm, stiff_ref)]
    pairs += [(velocity_hbm, velocity_ref)]
    pairs += [(read_hbm, read_ref), (moment_hbm, moment_ref), (solid_hbm, solid_ref)]
    loads = [
        pltpu.make_async_copy(src, dst, load_sems.at[i]) for i, (src, dst) in enumerate(pairs)
    ]
    for load in loads:
        load.start()
    depth, width = read_ref.shape[1], read_ref.shape[2]
    slots = states_ref.shape[1]
    vertices = states_ref.shape[2]
    tiles = vertices // 128
    quads = vertices // 256
    bx_count, by_count = width // 8, 16
    total = slots + 4 * MIG
    f32 = jnp.float32

    force_ref[...] = jnp.zeros_like(force_ref)
    for load in loads[:8]:
        load.wait()
    meta_row = MIG * tiles * 9 - meta_at
    last = MIG * tiles * 8
    for c in range(9):
        moved_ref[c, 0:slots, :] = states_ref[c]
        for j in range(tiles):
            at = j * 16 + 2 * c if c < 8 else last + 2 * j
            moved_ref[c, slots:total, j * 128 : (j + 1) * 128] = jnp.concatenate(
                [beads_ref[d, at : at + MIG, :] for d in range(4)], axis=0
            )
    count = jnp.int32(0)
    blocks = bricks_ref.shape[1]
    row16 = lax.broadcasted_iota(jnp.int32, (total, 128), 0)
    active = jnp.zeros((total, 128), jnp.int32)
    for s in range(total):
        slot_ref[count] = s
        if s < slots:
            here = jnp.where(leave_ref[0, s] == 0, 1, 0)
        else:
            d, m = divmod(s - slots, MIG)
            here = jnp.where(meta_ref[d, meta_row + m, blocks] > 0.5, 1, 0)
        count = count + here
        active = jnp.where(row16 == s, here, active)

    rows = moved_ref[3:6].reshape(3 * total, vertices).astype(jnp.bfloat16)
    loads[8].wait()
    for g in range(quads):
        part = jnp.dot(
            rows, stiff_ref[:, g * 256 : (g + 1) * 256], preferred_element_type=f32
        )
        node_ref[:, g * 256 : (g + 1) * 256] = -part

    loads[9].wait()
    sampled_ref[...] = jnp.zeros_like(sampled_ref)
    lane8 = lax.broadcasted_iota(jnp.int32, (8, 128), 1)
    row8 = lax.broadcasted_iota(jnp.int32, (8, 256), 0)
    steps8 = row8.astype(f32)
    group = lax.broadcasted_iota(jnp.int32, (8, 256), 1) // 64

    def couple(i, carry):
        s = slot_ref[i]
        own = s < slots
        inside = jnp.minimum(s, slots - 1)
        outside = jnp.maximum(s - slots, 0)
        for g in range(quads):
            cols = slice(g * 256, (g + 1) * 256)
            where = [
                jnp.where(
                    own,
                    bricks_ref[inside, 4 * g + j],
                    meta_ref[
                        outside // MIG, meta_row + outside % MIG, 4 * g + j
                    ].astype(jnp.int32),
                )
                for j in range(4)
            ]
            along_x = phi(moved_ref[0, pl.ds(s, 1), cols] - steps8)
            along_y = phi(moved_ref[1, pl.ds(s, 1), cols] - steps8)
            along_z = phi(moved_ref[2, pl.ds(s, 1), cols] - steps8)
            zx = [along_z[iz : iz + 1, :] * along_x for iz in range(8)]
            for k in range(4):
                for h in range(2):
                    iy = k + 4 * h
                    y_row = jnp.broadcast_to(along_y[iy : iy + 1, :], (8, 256))
                    for iz in range(0, 8, 2):
                        pair = jnp.concatenate([zx[iz] * y_row, zx[iz + 1] * y_row], axis=0)
                        at = (k * 2 + h) * 64 + iz * 8
                        weight_ref[g, at : at + 16, :] = pair.astype(jnp.bfloat16)
            near = jnp.concatenate(
                [
                    jnp.concatenate([velocity_ref[r, k] for k in range(4)], axis=1)
                    for r in where
                ],
                axis=0,
            ).astype(jnp.bfloat16)
            sampled = jnp.dot(near, weight_ref[g], preferred_element_type=f32)
            force = jnp.zeros((8, 256), f32)
            for c in range(3):
                force = jnp.where(row8 == c, node_ref[pl.ds(c * total + s, 1), cols], force)
            spreading = jnp.concatenate(
                [jnp.where(group == j, force, 0.0) for j in range(4)], axis=0
            ).astype(jnp.bfloat16)
            spread = lax.dot_general(
                spreading, weight_ref[g], (((1,), (1,)), ((), ())), preferred_element_type=f32
            )
            for j in range(4):
                for k in range(4):
                    force_ref[where[j], k] = (
                        force_ref[where[j], k]
                        + spread[8 * j : 8 * j + 8, k * 128 : (k + 1) * 128]
                    )
            vertex = jnp.zeros((8, 256), f32)
            for j in range(4):
                vertex = jnp.where(group == j, sampled[8 * j : 8 * j + 8, :], vertex)
            for c in range(3):
                sampled_ref[c, pl.ds(s, 1), cols] = vertex[c : c + 1, :]
        return carry

    lax.fori_loop(0, count, couple, 0)

    for j in range(tiles):
        cols = slice(j * 128, (j + 1) * 128)
        for c in range(3):
            speed = sampled_ref[c, :, cols]
            half = 0.5 * (moved_ref[6 + c, :, cols] + speed)
            vertex_ref[c, :, cols] = jnp.where(active > 0, moved_ref[c, :, cols] + half, 0.0)
            vertex_ref[3 + c, :, cols] = jnp.where(
                active > 0, moved_ref[3 + c, :, cols] + half, 0.0
            )
            vertex_ref[6 + c, :, cols] = speed
    finished = pltpu.make_async_copy(vertex_ref, vertex_out, sems.at[depth])
    finished.start()

    for load in loads[10:]:
        load.wait()
    for axis in range(3):
        for bz in range(depth // 8):
            parts = []
            for by in range(by_count):
                laid = []
                for bx in range(bx_count):
                    brick = (bz * bx_count + bx) * by_count + by
                    got = [force_ref[brick, k, axis : axis + 1, :] for k in range(4)]
                    laid.append(jnp.concatenate(got + got, axis=0))
                top = lax.broadcasted_iota(jnp.int32, (8, 128), 0) < 4
                low = jnp.where(top, laid[0], pltpu.roll(laid[0], 64, 1))
                high = jnp.where(top, pltpu.roll(laid[1], 64, 1), laid[1])
                parts.append(jnp.where(lane8 < 64, low, high))
            cells = jnp.concatenate(parts, axis=0).T
            for bx in range(bx_count):
                for iz in range(8):
                    at = (bx * 8 + iz) * 8
                    field_ref[axis, bz * 8 + iz, bx * 8 : bx * 8 + 8, :] = cells[at : at + 8, :]

    def collide(z, carry):
        density, inverse = moment_ref[0, z], moment_ref[4, z]
        force = [field_ref[axis, z] for axis in range(3)]
        speed = [(moment_ref[1 + axis, z] + 0.5 * force[axis]) * inverse for axis in range(3)]
        square = speed[0] * speed[0] + speed[1] * speed[1] + speed[2] * speed[2]
        dot = speed[0] * force[0] + speed[1] * force[1] + speed[2] * force[2]
        fluid = solid_ref[z] == 0
        base = (1.25 * density) * (1.0 - 1.5 * square) - 1.125 * dot
        dense = 5.625 * density
        odd = [3.75 * density * speed[axis] + 1.125 * force[axis] for axis in range(3)]
        slope = [3.375 * force[axis] for axis in range(3)]
        rest = read_ref[0, z]
        fresh_ref[0, z] = jnp.where(fluid, WEIGHTS[0] * base - 0.25 * rest, rest)

        def along(vector, c):
            terms = None
            for axis in range(3):
                if c[axis] == 0:
                    continue
                if terms is None:
                    terms = vector[axis] if c[axis] == 1 else -vector[axis]
                else:
                    terms = terms + vector[axis] if c[axis] == 1 else terms - vector[axis]
            return terms

        for q in range(1, 19, 2):
            c = LATTICE[q]
            e = along(speed, c)
            even = WEIGHTS[q] * (base + e * (dense * e + along(slope, c)))
            skew = WEIGHTS[q] * along(odd, c)
            ahead, back = read_ref[q, z], read_ref[q + 1, z]
            fresh_ref[q, z] = jnp.where(fluid, even + skew - 0.25 * ahead, back)
            fresh_ref[q + 1, z] = jnp.where(fluid, even - skew - 0.25 * back, ahead)
        pltpu.make_async_copy(fresh_ref.at[:, z], pops_out.at[:, z], sems.at[z]).start()
        return carry

    lax.fori_loop(0, depth, collide, 0)

    def finish(z, carry):
        pltpu.make_async_copy(fresh_ref.at[:, z], pops_out.at[:, z], sems.at[z]).wait()
        return carry

    lax.fori_loop(0, depth, finish, 0)
    finished.wait()


def advance(leaving, bricks, states, beads, solid, read, moment, velocity, stiffness):
    depth, width = read.shape[1], read.shape[2]
    slots, vertices = states.shape[1], states.shape[2]
    total = slots + 4 * MIG
    n_bricks = velocity.shape[0]
    hbm = pl.BlockSpec(memory_space=pltpu.HBM)
    f32 = jnp.float32
    return pl.pallas_call(
        step_kernel,
        out_shape=(
            jax.ShapeDtypeStruct(read.shape, f32),
            jax.ShapeDtypeStruct((9, total, vertices), f32),
        ),
        in_specs=[hbm] * 9,
        out_specs=(hbm, hbm),
        scratch_shapes=[
            pltpu.SMEM(leaving.shape, jnp.int32),
            pltpu.SMEM(bricks.shape, jnp.int32),
            pltpu.SMEM((4, 8, 128), f32),
            pltpu.VMEM(states.shape, f32),
            pltpu.VMEM(beads.shape, f32),
            pltpu.VMEM(solid.shape, jnp.int32),
            pltpu.VMEM(read.shape, f32),
            pltpu.VMEM(moment.shape, f32),
            pltpu.VMEM(velocity.shape, f32),
            pltpu.VMEM(stiffness.shape, stiffness.dtype),
            pltpu.VMEM(read.shape, f32),
            pltpu.VMEM((3, depth, width, 128), f32),
            pltpu.VMEM((n_bricks, 4, 8, 128), f32),
            pltpu.VMEM((9, total, vertices), f32),
            pltpu.VMEM((total * 3, vertices), f32),
            pltpu.VMEM((3, total, vertices), f32),
            pltpu.VMEM((9, total, vertices), f32),
            pltpu.VMEM((vertices // 256, 512, 256), jnp.bfloat16),
            pltpu.SMEM((total + 1,), jnp.int32),
            pltpu.SemaphoreType.DMA((depth + 1,)),
            pltpu.SemaphoreType.DMA((13,)),
        ],
        compiler_params=pltpu.CompilerParams(vmem_limit_bytes=56 * 1024 * 1024),
        name="step",
    )(leaving, bricks, states, beads, solid, read, moment, velocity, stiffness)


def solution(mesh):
    sizes = (mesh.shape["gx"], mesh.shape["gy"])

    def local(populations, solid_mask, bead_states, bead_bricks, leave_dir, stiffness):
        states = bead_states.reshape(bead_states.shape[2:]).transpose(1, 0, 2)
        bricks = bead_bricks.reshape(bead_bricks.shape[2:])
        leaving = leave_dir.reshape((1,) + leave_dir.shape[2:])
        beads, read, moment, velocity = exchange(
            populations, states, bricks, leaving, sizes
        )
        populations_out, vertex_out = advance(
            leaving, bricks, states, beads, solid_mask, read, moment, velocity, stiffness
        )
        vertex_out = vertex_out.transpose(1, 0, 2)
        return (populations_out, vertex_out.reshape((1, 1) + vertex_out.shape))

    return jax.shard_map(
        local,
        mesh=mesh,
        in_specs=(
            P(None, None, "gx", "gy"),
            P(None, "gx", "gy"),
            P("gx", "gy", None, None, None),
            P("gx", "gy", None, None),
            P("gx", "gy", None),
            P(),
        ),
        out_specs=(P(None, None, "gx", "gy"), P("gx", "gy", None, None, None)),
        check_vma=False,
    )
```

```python
import functools

import jax
import jax.numpy as jnp
import numpy as np
from jax import lax
from jax.experimental import pallas as pl
from jax.experimental.pallas import tpu as pltpu
from jax.sharding import PartitionSpec as P

MIG = 2
LATTICE = [
    (0, 0, 0),
    (1, 0, 0), (-1, 0, 0),
    (0, 1, 0), (0, -1, 0),
    (0, 0, 1), (0, 0, -1),
    (1, 1, 0), (-1, -1, 0),
    (1, -1, 0), (-1, 1, 0),
    (1, 0, 1), (-1, 0, -1),
    (1, 0, -1), (-1, 0, 1),
    (0, 1, 1), (0, -1, -1),
    (0, 1, -1), (0, -1, 1),
]
WEIGHTS = [1.0 / 3.0] + [1.0 / 18.0] * 6 + [1.0 / 36.0] * 12
X_UP = [q for q in range(19) if LATTICE[q][0] == 1]
X_DOWN = [q for q in range(19) if LATTICE[q][0] == -1]
Y_UP = [q for q in range(19) if LATTICE[q][1] == 1]
Y_DOWN = [q for q in range(19) if LATTICE[q][1] == -1]
MESH = pl.DeviceIdType.MESH
COS_FIT = [
    float(c)
    for c in np.polynomial.Chebyshev.interpolate(
        lambda u: np.cos(np.pi * np.sqrt(np.maximum(u, 0.0)) / 4.0), 5, domain=[0.0, 4.0]
    ).convert(kind=np.polynomial.Polynomial).coef
]


def exchange_kernel(
    sizes,
    leave_hbm,
    bricks_hbm,
    states_hbm,
    pops_hbm,
    beads_ref,
    read_hbm,
    moment_hbm,
    velocity_hbm,
    read_ref,
    moment_ref,
    velocity_ref,
    leave_ref,
    bricks_ref,
    states_ref,
    pops_ref,
    bead_out,
    x_out,
    y_out,
    xface_ref,
    yface_ref,
    corner_ref,
    diagonal_ref,
    field_ref,
    load_sems,
    store_sems,
    send_sems,
    recv_sems,
):
    n_gx, n_gy = sizes
    f32 = jnp.float32
    loads = [
        pltpu.make_async_copy(src, dst, load_sems.at[i])
        for i, (src, dst) in enumerate(
            (
                (leave_hbm, leave_ref),
                (bricks_hbm, bricks_ref),
                (states_hbm, states_ref),
                (pops_hbm, pops_ref),
            )
        )
    ]
    for load in loads:
        load.start()
    depth, width = pops_ref.shape[1], pops_ref.shape[2]
    slots = states_ref.shape[1]
    tiles = states_ref.shape[2] // 128
    blocks = bricks_ref.shape[1]
    bx_count, by_count = width // 8, 16
    ax, ay = lax.axis_index("gx"), lax.axis_index("gy")
    xp, xm = lax.rem(ax + 1, n_gx), lax.rem(ax + n_gx - 1, n_gx)
    yp, ym = lax.rem(ay + 1, n_gy), lax.rem(ay + n_gy - 1, n_gy)
    barrier = pltpu.get_barrier_semaphore()
    for where in ((xp, ay), (xm, ay), (ax, yp), (ax, ym), (xp, yp), (xm, ym), (xp, ym), (xm, yp)):
        pl.semaphore_signal(barrier, inc=1, device_id=where, device_id_type=MESH)

    for load in loads[:3]:
        load.wait()
    leaving = [leave_ref[0, s] for s in range(slots)]
    last = MIG * tiles * 8
    row = MIG * tiles * 9
    for d in (2, 3, 0, 1):
        first, second, count = jnp.int32(0), jnp.int32(0), jnp.int32(0)
        for s in range(slots):
            hit = leaving[s] == d + 1
            first = jnp.where(hit & (count == 0), s, first)
            second = jnp.where(hit & (count == 1), s, second)
            count = count + jnp.where(hit, 1, 0)
        for m, at in enumerate((first, second)):
            for c in range(9):
                line = states_ref[c, pl.ds(at, 1), :]
                for j in range(tiles):
                    to = j * 16 + 2 * c + m if c < 8 else last + 2 * j + m
                    bead_out[d, to : to + 1, :] = line[:, j * 128 : (j + 1) * 128]
            valid = jnp.where(count > m, 1.0, 0.0).astype(f32)
            bead_out[d, row + m : row + m + 1, :] = jnp.full((1, 128), valid, f32)
            bead_out[d, row + m : row + m + 1, 0:blocks] = bricks_ref[pl.ds(at, 1), :].astype(f32)

    loads[3].wait()
    for i, q in enumerate(X_UP):
        x_out[0, i] = pops_ref[q, :, width - 1, :]
    for i, q in enumerate(X_DOWN):
        x_out[1, i] = pops_ref[q, :, 0, :]
    lane = lax.broadcasted_iota(jnp.int32, (width, 128), 1)
    for side, (group, edge) in enumerate(((Y_UP, 127), (Y_DOWN, 0))):
        packed = jnp.zeros((width, 128), f32)
        for i, q in enumerate(group):
            for z in range(depth):
                t = i * depth + z
                packed = jnp.where(
                    lane == t, pltpu.roll(pops_ref[q, z], (t - edge) % 128, 1), packed
                )
        y_out[side] = packed

    pl.semaphore_wait(barrier, 8)
    copies = []

    def send(src, dst, where):
        at = len(copies)
        copy = pltpu.make_async_remote_copy(
            src_ref=src,
            dst_ref=dst,
            send_sem=send_sems.at[at],
            recv_sem=recv_sems.at[at],
            device_id=where,
            device_id_type=MESH,
        )
        copy.start()
        copies.append(copy)

    targets = ((xp, ay), (xm, ay), (ax, yp), (ax, ym))
    send(y_out.at[0], yface_ref.at[0], targets[2])
    send(y_out.at[1], yface_ref.at[1], targets[3])
    send(y_out.at[0, width - 8 : width], corner_ref.at[0], (xp, yp))
    send(y_out.at[1, 0:8], corner_ref.at[1], (xm, ym))
    send(y_out.at[1, width - 8 : width], corner_ref.at[2], (xp, ym))
    send(y_out.at[0, 0:8], corner_ref.at[3], (xm, yp))
    send(x_out.at[0], xface_ref.at[0], targets[0])
    send(x_out.at[1], xface_ref.at[1], targets[1])
    for d in (2, 3, 0, 1):
        send(bead_out.at[d], beads_ref.at[d], targets[d])
    for copy in copies[:8]:
        copy.wait_recv()

    row8 = lax.broadcasted_iota(jnp.int32, (width, 128), 0)
    for i, (side, up) in enumerate(((0, True), (1, False), (1, True), (0, False))):
        face = yface_ref[side]
        if up:
            edge = jnp.broadcast_to(corner_ref[i, 7:8, :], (width, 128))
            diagonal_ref[i] = jnp.where(row8 == 0, edge, pltpu.roll(face, 1, 0))
        else:
            edge = jnp.broadcast_to(corner_ref[i, 0:1, :], (width, 128))
            diagonal_ref[i] = jnp.where(row8 == width - 1, edge, pltpu.roll(face, width - 1, 0))

    def pull(z, carry):
        density = None
        sums = [None, None, None]
        for q in range(19):
            cx, cy, cz = LATTICE[q]
            zs = z if cz == 0 else lax.rem(z - cz + depth, depth)
            value = pops_ref[q, zs]
            if cx == 1:
                edge = xface_ref[0, X_UP.index(q), pl.ds(zs, 1), :]
                value = jnp.where(row8 == 0, edge, pltpu.roll(value, 1, 0))
            elif cx == -1:
                edge = xface_ref[1, X_DOWN.index(q), pl.ds(zs, 1), :]
                value = jnp.where(row8 == width - 1, edge, pltpu.roll(value, width - 1, 0))
            if cy != 0:
                face = diagonal_ref[q - 7] if cx != 0 else yface_ref[0 if cy == 1 else 1]
                t = (Y_UP if cy == 1 else Y_DOWN).index(q) * depth + zs
                if cy == 1:
                    edge = pltpu.roll(face, lax.rem(128 - t, 128), 1)
                    value = jnp.where(lane == 0, edge, pltpu.roll(value, 1, 1))
                else:
                    edge = pltpu.roll(face, 127 - t, 1)
                    value = jnp.where(lane == 127, edge, pltpu.roll(value, 127, 1))
            read_ref[q, z] = value
            density = value if density is None else density + value
            for axis, c in enumerate((cx, cy, cz)):
                if c == 1:
                    sums[axis] = value if sums[axis] is None else sums[axis] + value
                elif c == -1:
                    sums[axis] = sums[axis] - value
        inverse = 1.0 / density
        moment_ref[0, z] = density
        moment_ref[4, z] = inverse
        for axis in range(3):
            moment_ref[1 + axis, z] = sums[axis]
            field_ref[axis, z] = (sums[axis] * inverse).astype(jnp.bfloat16).astype(f32)
        pltpu.make_async_copy(read_ref.at[:, z], read_hbm.at[:, z], store_sems.at[z]).start()
        return carry

    lax.fori_loop(0, depth, pull, 0)
    stored = pltpu.make_async_copy(moment_ref, moment_hbm, store_sems.at[depth])
    stored.start()

    for axis in range(3):
        for bz in range(depth // 8):
            cells = jnp.concatenate(
                [
                    field_ref[axis, bz * 8 + iz, bx * 8 : bx * 8 + 8, :]
                    for bx in range(bx_count)
                    for iz in range(8)
                ],
                axis=0,
            )
            turned = cells.T
            for bx in range(bx_count):
                laid = turned if bx == 0 else pltpu.roll(turned, 64, 1)
                for by in range(by_count):
                    brick = (bz * bx_count + bx) * by_count + by
                    velocity_ref[brick, axis * 8 : axis * 8 + 8, :] = laid[by * 8 : by * 8 + 8, :]

    laid_out = pltpu.make_async_copy(velocity_ref, velocity_hbm, store_sems.at[depth + 1])
    laid_out.start()

    def finish(z, carry):
        pltpu.make_async_copy(read_ref.at[:, z], read_hbm.at[:, z], store_sems.at[z]).wait()
        return carry

    lax.fori_loop(0, depth, finish, 0)
    stored.wait()
    for copy in copies[:8]:
        copy.wait_send()
    for copy in copies[8:]:
        copy.wait()
    laid_out.wait()


def exchange(populations, states, bricks, leaving, sizes):
    depth, width = populations.shape[1], populations.shape[2]
    tiles = states.shape[2] // 128
    rows = -(-MIG * (tiles * 9 + 1) // 8) * 8
    n_bricks = (depth // 8) * (width // 8) * 16
    hbm = pl.BlockSpec(memory_space=pltpu.HBM)
    f32 = jnp.float32
    return pl.pallas_call(
        functools.partial(exchange_kernel, sizes),
        out_shape=(
            jax.ShapeDtypeStruct((4, rows, 128), f32),
            jax.ShapeDtypeStruct(populations.shape, f32),
            jax.ShapeDtypeStruct((5, depth, width, 128), f32),
            jax.ShapeDtypeStruct((n_bricks, 24, 128), f32),
        ),
        in_specs=[hbm] * 4,
        out_specs=(hbm,) * 4,
        scratch_shapes=[
            pltpu.VMEM(populations.shape, f32),
            pltpu.VMEM((5, depth, width, 128), f32),
            pltpu.VMEM((n_bricks, 24, 128), f32),
            pltpu.SMEM(leaving.shape, jnp.int32),
            pltpu.VMEM(bricks.shape, jnp.int32),
            pltpu.VMEM(states.shape, f32),
            pltpu.VMEM(populations.shape, f32),
            pltpu.VMEM((4, rows, 128), f32),
            pltpu.VMEM((2, 5, depth, 128), f32),
            pltpu.VMEM((2, width, 128), f32),
            pltpu.VMEM((2, 5, depth, 128), f32),
            pltpu.VMEM((2, width, 128), f32),
            pltpu.VMEM((4, 8, 128), f32),
            pltpu.VMEM((4, width, 128), f32),
            pltpu.VMEM((3, depth, width, 128), f32),
            pltpu.SemaphoreType.DMA((4,)),
            pltpu.SemaphoreType.DMA((depth + 2,)),
            pltpu.SemaphoreType.DMA((12,)),
            pltpu.SemaphoreType.DMA((12,)),
        ],
        compiler_params=pltpu.CompilerParams(
            collective_id=0, has_side_effects=True, vmem_limit_bytes=56 * 1024 * 1024
        ),
        name="exchange",
    )(leaving, bricks, states, populations)


def phi(distance):
    square = distance * distance
    u = jnp.minimum(square, 4.0)
    value = jnp.full_like(u, COS_FIT[5])
    for c in COS_FIT[4::-1]:
        value = value * u + c
    return jnp.where(square < 4.0, 0.5 * value * value, 0.0)


def step_kernel(
    leave_hbm,
    bricks_hbm,
    states_hbm,
    beads_hbm,
    solid_hbm,
    read_hbm,
    moment_hbm,
    velocity_hbm,
    stiff_hbm,
    pops_out,
    vertex_out,
    leave_ref,
    bricks_ref,
    meta_ref,
    states_ref,
    beads_ref,
    solid_ref,
    read_ref,
    moment_ref,
    velocity_ref,
    stiff_ref,
    fresh_ref,
    field_ref,
    force_ref,
    moved_ref,
    node_ref,
    sampled_ref,
    vertex_ref,
    weight_ref,
    slot_ref,
    sems,
    load_sems,
):
    meta_at = beads_hbm.shape[1] - 8
    pairs = [(leave_hbm, leave_ref), (bricks_hbm, bricks_ref)]
    pairs += [(beads_hbm.at[d, meta_at : meta_at + 8], meta_ref.at[d]) for d in range(4)]
    pairs += [(states_hbm, states_ref), (beads_hbm, beads_ref), (stiff_hbm, stiff_ref)]
    pairs += [(velocity_hbm, velocity_ref)]
    pairs += [(read_hbm, read_ref), (moment_hbm, moment_ref), (solid_hbm, solid_ref)]
    loads = [
        pltpu.make_async_copy(src, dst, load_sems.at[i]) for i, (src, dst) in enumerate(pairs)
    ]
    for load in loads:
        load.start()
    depth, width = read_ref.shape[1], read_ref.shape[2]
    slots = states_ref.shape[1]
    vertices = states_ref.shape[2]
    tiles = vertices // 128
    quads = vertices // 256
    bx_count, by_count = width // 8, 16
    total = slots + 4 * MIG
    f32 = jnp.float32

    force_ref[...] = jnp.zeros_like(force_ref)
    for load in loads[:8]:
        load.wait()
    meta_row = MIG * tiles * 9 - meta_at
    last = MIG * tiles * 8
    for c in range(9):
        moved_ref[c, 0:slots, :] = states_ref[c]
        for j in range(tiles):
            at = j * 16 + 2 * c if c < 8 else last + 2 * j
            moved_ref[c, slots:total, j * 128 : (j + 1) * 128] = jnp.concatenate(
                [beads_ref[d, at : at + MIG, :] for d in range(4)], axis=0
            )
    count = jnp.int32(0)
    blocks = bricks_ref.shape[1]
    row16 = lax.broadcasted_iota(jnp.int32, (total, 128), 0)
    active = jnp.zeros((total, 128), jnp.int32)
    for s in range(total):
        slot_ref[count] = s
        if s < slots:
            here = jnp.where(leave_ref[0, s] == 0, 1, 0)
        else:
            d, m = divmod(s - slots, MIG)
            here = jnp.where(meta_ref[d, meta_row + m, blocks] > 0.5, 1, 0)
        count = count + here
        active = jnp.where(row16 == s, here, active)

    rows = moved_ref[3:6].reshape(3 * total, vertices).astype(jnp.bfloat16)
    loads[8].wait()
    for g in range(quads):
        part = jnp.dot(
            rows, stiff_ref[:, g * 256 : (g + 1) * 256], preferred_element_type=f32
        )
        node_ref[:, g * 256 : (g + 1) * 256] = -part

    loads[9].wait()
    sampled_ref[...] = jnp.zeros_like(sampled_ref)
    lane8 = lax.broadcasted_iota(jnp.int32, (8, 128), 1)
    row8 = lax.broadcasted_iota(jnp.int32, (8, 256), 0)
    steps8 = row8.astype(f32)
    group = lax.broadcasted_iota(jnp.int32, (8, 256), 1) // 64

    def couple(i, carry):
        s = slot_ref[i]
        own = s < slots
        inside = jnp.minimum(s, slots - 1)
        outside = jnp.maximum(s - slots, 0)
        for g in range(quads):
            cols = slice(g * 256, (g + 1) * 256)
            where = [
                jnp.where(
                    own,
                    bricks_ref[inside, 4 * g + j],
                    meta_ref[
                        outside // MIG, meta_row + outside % MIG, 4 * g + j
                    ].astype(jnp.int32),
                )
                for j in range(4)
            ]
            along_x = phi(moved_ref[0, pl.ds(s, 1), cols] - steps8)
            along_y = phi(moved_ref[1, pl.ds(s, 1), cols] - steps8)
            along_z = phi(moved_ref[2, pl.ds(s, 1), cols] - steps8)
            zx = [along_z[iz : iz + 1, :] * along_x for iz in range(8)]
            for k in range(4):
                for h in range(2):
                    iy = k + 4 * h
                    y_row = jnp.broadcast_to(along_y[iy : iy + 1, :], (8, 256))
                    for iz in range(0, 8, 2):
                        pair = jnp.concatenate([zx[iz] * y_row, zx[iz + 1] * y_row], axis=0)
                        at = (k * 2 + h) * 64 + iz * 8
                        weight_ref[g, at : at + 16, :] = pair.astype(jnp.bfloat16)
            near = jnp.concatenate([velocity_ref[r] for r in where], axis=0)
            flat = jnp.concatenate(zx, axis=0).astype(jnp.bfloat16)
            sampled = jnp.dot(
                near[:, 0:64].astype(jnp.bfloat16), flat, preferred_element_type=f32
            )
            for c in range(3):
                vertex = sampled[8 * c : 8 * c + 8, :]
                for j in range(1, 4):
                    at = 24 * j + 8 * c
                    vertex = jnp.where(group == j, sampled[at : at + 8, :], vertex)
                sampled_ref[c, pl.ds(s, 1), cols] = jnp.sum(
                    vertex * along_y, axis=0, keepdims=True
                )
            force = jnp.zeros((8, 256), f32)
            for c in range(3):
                force = jnp.where(row8 == c, node_ref[pl.ds(c * total + s, 1), cols], force)
            spreading = jnp.concatenate(
                [jnp.where(group == j, force, 0.0) for j in range(4)], axis=0
            ).astype(jnp.bfloat16)
            spread = lax.dot_general(
                spreading, weight_ref[g], (((1,), (1,)), ((), ())), preferred_element_type=f32
            )
            for j in range(4):
                for k in range(4):
                    force_ref[where[j], k] = (
                        force_ref[where[j], k]
                        + spread[8 * j : 8 * j + 8, k * 128 : (k + 1) * 128]
                    )
        return carry

    lax.fori_loop(0, count, couple, 0)

    for j in range(tiles):
        cols = slice(j * 128, (j + 1) * 128)
        for c in range(3):
            speed = sampled_ref[c, :, cols]
            half = 0.5 * (moved_ref[6 + c, :, cols] + speed)
            vertex_ref[c, :, cols] = jnp.where(active > 0, moved_ref[c, :, cols] + half, 0.0)
            vertex_ref[3 + c, :, cols] = jnp.where(
                active > 0, moved_ref[3 + c, :, cols] + half, 0.0
            )
            vertex_ref[6 + c, :, cols] = speed
    finished = pltpu.make_async_copy(vertex_ref, vertex_out, sems.at[depth])
    finished.start()

    for load in loads[10:]:
        load.wait()
    for axis in range(3):
        for bz in range(depth // 8):
            parts = []
            for by in range(by_count):
                laid = []
                for bx in range(bx_count):
                    brick = (bz * bx_count + bx) * by_count + by
                    got = [force_ref[brick, k, axis : axis + 1, :] for k in range(4)]
                    laid.append(jnp.concatenate(got + got, axis=0))
                top = lax.broadcasted_iota(jnp.int32, (8, 128), 0) < 4
                low = jnp.where(top, laid[0], pltpu.roll(laid[0], 64, 1))
                high = jnp.where(top, pltpu.roll(laid[1], 64, 1), laid[1])
                parts.append(jnp.where(lane8 < 64, low, high))
            cells = jnp.concatenate(parts, axis=0).T
            for bx in range(bx_count):
                for iz in range(8):
                    at = (bx * 8 + iz) * 8
                    field_ref[axis, bz * 8 + iz, bx * 8 : bx * 8 + 8, :] = cells[at : at + 8, :]

    def collide(z, carry):
        density, inverse = moment_ref[0, z], moment_ref[4, z]
        force = [field_ref[axis, z] for axis in range(3)]
        speed = [(moment_ref[1 + axis, z] + 0.5 * force[axis]) * inverse for axis in range(3)]
        square = speed[0] * speed[0] + speed[1] * speed[1] + speed[2] * speed[2]
        dot = speed[0] * force[0] + speed[1] * force[1] + speed[2] * force[2]
        fluid = solid_ref[z] == 0
        base = (1.25 * density) * (1.0 - 1.5 * square) - 1.125 * dot
        dense = 5.625 * density
        odd = [3.75 * density * speed[axis] + 1.125 * force[axis] for axis in range(3)]
        slope = [3.375 * force[axis] for axis in range(3)]
        rest = read_ref[0, z]
        fresh_ref[0, z] = jnp.where(fluid, WEIGHTS[0] * base - 0.25 * rest, rest)

        def along(vector, c):
            terms = None
            for axis in range(3):
                if c[axis] == 0:
                    continue
                if terms is None:
                    terms = vector[axis] if c[axis] == 1 else -vector[axis]
                else:
                    terms = terms + vector[axis] if c[axis] == 1 else terms - vector[axis]
            return terms

        for q in range(1, 19, 2):
            c = LATTICE[q]
            e = along(speed, c)
            even = WEIGHTS[q] * (base + e * (dense * e + along(slope, c)))
            skew = WEIGHTS[q] * along(odd, c)
            ahead, back = read_ref[q, z], read_ref[q + 1, z]
            fresh_ref[q, z] = jnp.where(fluid, even + skew - 0.25 * ahead, back)
            fresh_ref[q + 1, z] = jnp.where(fluid, even - skew - 0.25 * back, ahead)
        pltpu.make_async_copy(fresh_ref.at[:, z], pops_out.at[:, z], sems.at[z]).start()
        return carry

    lax.fori_loop(0, depth, collide, 0)

    def finish(z, carry):
        pltpu.make_async_copy(fresh_ref.at[:, z], pops_out.at[:, z], sems.at[z]).wait()
        return carry

    lax.fori_loop(0, depth, finish, 0)
    finished.wait()


def advance(leaving, bricks, states, beads, solid, read, moment, velocity, stiffness):
    depth, width = read.shape[1], read.shape[2]
    slots, vertices = states.shape[1], states.shape[2]
    total = slots + 4 * MIG
    n_bricks = velocity.shape[0]
    hbm = pl.BlockSpec(memory_space=pltpu.HBM)
    f32 = jnp.float32
    return pl.pallas_call(
        step_kernel,
        out_shape=(
            jax.ShapeDtypeStruct(read.shape, f32),
            jax.ShapeDtypeStruct((9, total, vertices), f32),
        ),
        in_specs=[hbm] * 9,
        out_specs=(hbm, hbm),
        scratch_shapes=[
            pltpu.SMEM(leaving.shape, jnp.int32),
            pltpu.SMEM(bricks.shape, jnp.int32),
            pltpu.SMEM((4, 8, 128), f32),
            pltpu.VMEM(states.shape, f32),
            pltpu.VMEM(beads.shape, f32),
            pltpu.VMEM(solid.shape, jnp.int32),
            pltpu.VMEM(read.shape, f32),
            pltpu.VMEM(moment.shape, f32),
            pltpu.VMEM(velocity.shape, f32),
            pltpu.VMEM(stiffness.shape, stiffness.dtype),
            pltpu.VMEM(read.shape, f32),
            pltpu.VMEM((3, depth, width, 128), f32),
            pltpu.VMEM((n_bricks, 4, 8, 128), f32),
            pltpu.VMEM((9, total, vertices), f32),
            pltpu.VMEM((total * 3, vertices), f32),
            pltpu.VMEM((3, total, vertices), f32),
            pltpu.VMEM((9, total, vertices), f32),
            pltpu.VMEM((vertices // 256, 512, 256), jnp.bfloat16),
            pltpu.SMEM((total + 1,), jnp.int32),
            pltpu.SemaphoreType.DMA((depth + 1,)),
            pltpu.SemaphoreType.DMA((13,)),
        ],
        compiler_params=pltpu.CompilerParams(vmem_limit_bytes=56 * 1024 * 1024),
        name="step",
    )(leaving, bricks, states, beads, solid, read, moment, velocity, stiffness)


def solution(mesh):
    sizes = (mesh.shape["gx"], mesh.shape["gy"])

    def local(populations, solid_mask, bead_states, bead_bricks, leave_dir, stiffness):
        states = bead_states.reshape(bead_states.shape[2:]).transpose(1, 0, 2)
        bricks = bead_bricks.reshape(bead_bricks.shape[2:])
        leaving = leave_dir.reshape((1,) + leave_dir.shape[2:])
        beads, read, moment, velocity = exchange(
            populations, states, bricks, leaving, sizes
        )
        populations_out, vertex_out = advance(
            leaving, bricks, states, beads, solid_mask, read, moment, velocity, stiffness
        )
        vertex_out = vertex_out.transpose(1, 0, 2)
        return (populations_out, vertex_out.reshape((1, 1) + vertex_out.shape))

    return jax.shard_map(
        local,
        mesh=mesh,
        in_specs=(
            P(None, None, "gx", "gy"),
            P(None, "gx", "gy"),
            P("gx", "gy", None, None, None),
            P("gx", "gy", None, None),
            P("gx", "gy", None),
            P(),
        ),
        out_specs=(P(None, None, "gx", "gy"), P("gx", "gy", None, None, None)),
        check_vma=False,
    )
```

```python
import functools

import jax
import jax.numpy as jnp
import numpy as np
from jax import lax
from jax.experimental import pallas as pl
from jax.experimental.pallas import tpu as pltpu
from jax.sharding import PartitionSpec as P

MIG = 2
LATTICE = [
    (0, 0, 0),
    (1, 0, 0), (-1, 0, 0),
    (0, 1, 0), (0, -1, 0),
    (0, 0, 1), (0, 0, -1),
    (1, 1, 0), (-1, -1, 0),
    (1, -1, 0), (-1, 1, 0),
    (1, 0, 1), (-1, 0, -1),
    (1, 0, -1), (-1, 0, 1),
    (0, 1, 1), (0, -1, -1),
    (0, 1, -1), (0, -1, 1),
]
WEIGHTS = [1.0 / 3.0] + [1.0 / 18.0] * 6 + [1.0 / 36.0] * 12
X_UP = [q for q in range(19) if LATTICE[q][0] == 1]
X_DOWN = [q for q in range(19) if LATTICE[q][0] == -1]
Y_UP = [q for q in range(19) if LATTICE[q][1] == 1]
Y_DOWN = [q for q in range(19) if LATTICE[q][1] == -1]
MESH = pl.DeviceIdType.MESH
COS_FIT = [
    float(c)
    for c in np.polynomial.Chebyshev.interpolate(
        lambda u: np.cos(np.pi * np.sqrt(np.maximum(u, 0.0)) / 4.0), 5, domain=[0.0, 4.0]
    ).convert(kind=np.polynomial.Polynomial).coef
]


def exchange_kernel(
    sizes,
    leave_hbm,
    bricks_hbm,
    states_hbm,
    pops_hbm,
    beads_ref,
    read_hbm,
    moment_hbm,
    velocity_hbm,
    read_ref,
    moment_ref,
    velocity_ref,
    leave_ref,
    bricks_ref,
    states_ref,
    pops_ref,
    bead_out,
    x_out,
    y_out,
    xface_ref,
    yface_ref,
    corner_ref,
    diagonal_ref,
    field_ref,
    load_sems,
    store_sems,
    send_sems,
    recv_sems,
):
    n_gx, n_gy = sizes
    f32 = jnp.float32
    loads = [
        pltpu.make_async_copy(src, dst, load_sems.at[i])
        for i, (src, dst) in enumerate(
            (
                (leave_hbm, leave_ref),
                (bricks_hbm, bricks_ref),
                (states_hbm, states_ref),
                (pops_hbm, pops_ref),
            )
        )
    ]
    for load in loads:
        load.start()
    depth, width = pops_ref.shape[1], pops_ref.shape[2]
    slots = states_ref.shape[1]
    tiles = states_ref.shape[2] // 128
    blocks = bricks_ref.shape[1]
    bx_count, by_count = width // 8, 16
    ax, ay = lax.axis_index("gx"), lax.axis_index("gy")
    xp, xm = lax.rem(ax + 1, n_gx), lax.rem(ax + n_gx - 1, n_gx)
    yp, ym = lax.rem(ay + 1, n_gy), lax.rem(ay + n_gy - 1, n_gy)
    barrier = pltpu.get_barrier_semaphore()
    for where in ((xp, ay), (xm, ay), (ax, yp), (ax, ym), (xp, yp), (xm, ym), (xp, ym), (xm, yp)):
        pl.semaphore_signal(barrier, inc=1, device_id=where, device_id_type=MESH)

    for load in loads[:3]:
        load.wait()
    leaving = [leave_ref[0, s] for s in range(slots)]
    copies = []

    def send(src, dst, where):
        at = len(copies)
        copy = pltpu.make_async_remote_copy(
            src_ref=src,
            dst_ref=dst,
            send_sem=send_sems.at[at],
            recv_sem=recv_sems.at[at],
            device_id=where,
            device_id_type=MESH,
        )
        copy.start()
        copies.append(copy)
        return copy

    targets = ((xp, ay), (xm, ay), (ax, yp), (ax, ym))
    last = MIG * tiles * 8
    row = MIG * tiles * 9
    for d in (2, 0, 3, 1):
        first, second, count = jnp.int32(0), jnp.int32(0), jnp.int32(0)
        for s in range(slots):
            hit = leaving[s] == d + 1
            first = jnp.where(hit & (count == 0), s, first)
            second = jnp.where(hit & (count == 1), s, second)
            count = count + jnp.where(hit, 1, 0)
        for m, at in enumerate((first, second)):
            for c in range(9):
                line = states_ref[c, pl.ds(at, 1), :]
                for j in range(tiles):
                    to = j * 16 + 2 * c + m if c < 8 else last + 2 * j + m
                    bead_out[d, to : to + 1, :] = line[:, j * 128 : (j + 1) * 128]
            valid = jnp.where(count > m, 1.0, 0.0).astype(f32)
            bead_out[d, row + m : row + m + 1, :] = jnp.full((1, 128), valid, f32)
            bead_out[d, row + m : row + m + 1, 0:blocks] = bricks_ref[pl.ds(at, 1), :].astype(f32)
        if d == 2:
            pl.semaphore_wait(barrier, 8)
        if d in (2, 0):
            send(bead_out.at[d], beads_ref.at[d], targets[d])

    loads[3].wait()
    for i, q in enumerate(X_UP):
        x_out[0, i] = pops_ref[q, :, width - 1, :]
    for i, q in enumerate(X_DOWN):
        x_out[1, i] = pops_ref[q, :, 0, :]
    lane = lax.broadcasted_iota(jnp.int32, (width, 128), 1)
    for side, (group, edge) in enumerate(((Y_UP, 127), (Y_DOWN, 0))):
        packed = jnp.zeros((width, 128), f32)
        for i, q in enumerate(group):
            for z in range(depth):
                t = i * depth + z
                packed = jnp.where(
                    lane == t, pltpu.roll(pops_ref[q, z], (t - edge) % 128, 1), packed
                )
        y_out[side] = packed

    faces = [
        send(y_out.at[0], yface_ref.at[0], targets[2]),
        send(y_out.at[1], yface_ref.at[1], targets[3]),
        send(y_out.at[0, width - 8 : width], corner_ref.at[0], (xp, yp)),
        send(y_out.at[1, 0:8], corner_ref.at[1], (xm, ym)),
        send(y_out.at[1, width - 8 : width], corner_ref.at[2], (xp, ym)),
        send(y_out.at[0, 0:8], corner_ref.at[3], (xm, yp)),
        send(x_out.at[0], xface_ref.at[0], targets[0]),
        send(x_out.at[1], xface_ref.at[1], targets[1]),
    ]
    for d in (3, 1):
        send(bead_out.at[d], beads_ref.at[d], targets[d])
    for copy in faces:
        copy.wait_recv()

    row8 = lax.broadcasted_iota(jnp.int32, (width, 128), 0)
    for i, (side, up) in enumerate(((0, True), (1, False), (1, True), (0, False))):
        face = yface_ref[side]
        if up:
            edge = jnp.broadcast_to(corner_ref[i, 7:8, :], (width, 128))
            diagonal_ref[i] = jnp.where(row8 == 0, edge, pltpu.roll(face, 1, 0))
        else:
            edge = jnp.broadcast_to(corner_ref[i, 0:1, :], (width, 128))
            diagonal_ref[i] = jnp.where(row8 == width - 1, edge, pltpu.roll(face, width - 1, 0))

    def pull(z, carry):
        density = None
        sums = [None, None, None]
        for q in range(19):
            cx, cy, cz = LATTICE[q]
            zs = z if cz == 0 else lax.rem(z - cz + depth, depth)
            value = pops_ref[q, zs]
            if cx == 1:
                edge = xface_ref[0, X_UP.index(q), pl.ds(zs, 1), :]
                value = jnp.where(row8 == 0, edge, pltpu.roll(value, 1, 0))
            elif cx == -1:
                edge = xface_ref[1, X_DOWN.index(q), pl.ds(zs, 1), :]
                value = jnp.where(row8 == width - 1, edge, pltpu.roll(value, width - 1, 0))
            if cy != 0:
                face = diagonal_ref[q - 7] if cx != 0 else yface_ref[0 if cy == 1 else 1]
                t = (Y_UP if cy == 1 else Y_DOWN).index(q) * depth + zs
                if cy == 1:
                    edge = pltpu.roll(face, lax.rem(128 - t, 128), 1)
                    value = jnp.where(lane == 0, edge, pltpu.roll(value, 1, 1))
                else:
                    edge = pltpu.roll(face, 127 - t, 1)
                    value = jnp.where(lane == 127, edge, pltpu.roll(value, 127, 1))
            read_ref[q, z] = value
            density = value if density is None else density + value
            for axis, c in enumerate((cx, cy, cz)):
                if c == 1:
                    sums[axis] = value if sums[axis] is None else sums[axis] + value
                elif c == -1:
                    sums[axis] = sums[axis] - value
        inverse = 1.0 / density
        moment_ref[0, z] = density
        moment_ref[4, z] = inverse
        for axis in range(3):
            moment_ref[1 + axis, z] = sums[axis]
            field_ref[axis, z] = (sums[axis] * inverse).astype(jnp.bfloat16).astype(f32)
        pltpu.make_async_copy(read_ref.at[:, z], read_hbm.at[:, z], store_sems.at[z]).start()
        return carry

    lax.fori_loop(0, depth, pull, 0)
    stored = pltpu.make_async_copy(moment_ref, moment_hbm, store_sems.at[depth])
    stored.start()

    for axis in range(3):
        for bz in range(depth // 8):
            cells = jnp.concatenate(
                [
                    field_ref[axis, bz * 8 + iz, bx * 8 : bx * 8 + 8, :]
                    for bx in range(bx_count)
                    for iz in range(8)
                ],
                axis=0,
            )
            turned = cells.T
            for bx in range(bx_count):
                laid = turned if bx == 0 else pltpu.roll(turned, 64, 1)
                for by in range(by_count):
                    brick = (bz * bx_count + bx) * by_count + by
                    velocity_ref[brick, axis * 8 : axis * 8 + 8, :] = laid[by * 8 : by * 8 + 8, :]

    laid_out = pltpu.make_async_copy(velocity_ref, velocity_hbm, store_sems.at[depth + 1])
    laid_out.start()

    def finish(z, carry):
        pltpu.make_async_copy(read_ref.at[:, z], read_hbm.at[:, z], store_sems.at[z]).wait()
        return carry

    lax.fori_loop(0, depth, finish, 0)
    stored.wait()
    for copy in copies:
        copy.wait_send()
    for copy in copies:
        if not any(copy is face for face in faces):
            copy.wait_recv()
    laid_out.wait()


def exchange(populations, states, bricks, leaving, sizes):
    depth, width = populations.shape[1], populations.shape[2]
    tiles = states.shape[2] // 128
    rows = -(-MIG * (tiles * 9 + 1) // 8) * 8
    n_bricks = (depth // 8) * (width // 8) * 16
    hbm = pl.BlockSpec(memory_space=pltpu.HBM)
    f32 = jnp.float32
    return pl.pallas_call(
        functools.partial(exchange_kernel, sizes),
        out_shape=(
            jax.ShapeDtypeStruct((4, rows, 128), f32),
            jax.ShapeDtypeStruct(populations.shape, f32),
            jax.ShapeDtypeStruct((5, depth, width, 128), f32),
            jax.ShapeDtypeStruct((n_bricks, 24, 128), f32),
        ),
        in_specs=[hbm] * 4,
        out_specs=(hbm,) * 4,
        scratch_shapes=[
            pltpu.VMEM(populations.shape, f32),
            pltpu.VMEM((5, depth, width, 128), f32),
            pltpu.VMEM((n_bricks, 24, 128), f32),
            pltpu.SMEM(leaving.shape, jnp.int32),
            pltpu.VMEM(bricks.shape, jnp.int32),
            pltpu.VMEM(states.shape, f32),
            pltpu.VMEM(populations.shape, f32),
            pltpu.VMEM((4, rows, 128), f32),
            pltpu.VMEM((2, 5, depth, 128), f32),
            pltpu.VMEM((2, width, 128), f32),
            pltpu.VMEM((2, 5, depth, 128), f32),
            pltpu.VMEM((2, width, 128), f32),
            pltpu.VMEM((4, 8, 128), f32),
            pltpu.VMEM((4, width, 128), f32),
            pltpu.VMEM((3, depth, width, 128), f32),
            pltpu.SemaphoreType.DMA((4,)),
            pltpu.SemaphoreType.DMA((depth + 2,)),
            pltpu.SemaphoreType.DMA((12,)),
            pltpu.SemaphoreType.DMA((12,)),
        ],
        compiler_params=pltpu.CompilerParams(
            collective_id=0, has_side_effects=True, vmem_limit_bytes=56 * 1024 * 1024
        ),
        name="exchange",
    )(leaving, bricks, states, populations)


def phi(distance):
    square = distance * distance
    u = jnp.minimum(square, 4.0)
    value = jnp.full_like(u, COS_FIT[5])
    for c in COS_FIT[4::-1]:
        value = value * u + c
    return jnp.where(square < 4.0, 0.5 * value * value, 0.0)


def step_kernel(
    leave_hbm,
    bricks_hbm,
    states_hbm,
    beads_hbm,
    solid_hbm,
    read_hbm,
    moment_hbm,
    velocity_hbm,
    stiff_hbm,
    pops_out,
    vertex_out,
    leave_ref,
    bricks_ref,
    meta_ref,
    states_ref,
    beads_ref,
    solid_ref,
    read_ref,
    moment_ref,
    velocity_ref,
    stiff_ref,
    fresh_ref,
    field_ref,
    force_ref,
    moved_ref,
    node_ref,
    sampled_ref,
    vertex_ref,
    weight_ref,
    slot_ref,
    sems,
    load_sems,
):
    meta_at = beads_hbm.shape[1] - 8
    pairs = [(leave_hbm, leave_ref), (bricks_hbm, bricks_ref)]
    pairs += [(beads_hbm.at[d, meta_at : meta_at + 8], meta_ref.at[d]) for d in range(4)]
    pairs += [(states_hbm, states_ref), (beads_hbm, beads_ref)]
    parts = stiff_hbm.shape[1] // 256
    for g in range(parts):
        cols = slice(g * 256, (g + 1) * 256)
        pairs += [(stiff_hbm.at[:, cols], stiff_ref.at[:, cols])]
    pairs += [(velocity_hbm, velocity_ref)]
    pairs += [(read_hbm, read_ref), (moment_hbm, moment_ref), (solid_hbm, solid_ref)]
    loads = [
        pltpu.make_async_copy(src, dst, load_sems.at[i]) for i, (src, dst) in enumerate(pairs)
    ]
    for load in loads:
        load.start()
    depth, width = read_ref.shape[1], read_ref.shape[2]
    slots = states_ref.shape[1]
    vertices = states_ref.shape[2]
    tiles = vertices // 128
    quads = vertices // 256
    bx_count, by_count = width // 8, 16
    total = slots + 4 * MIG
    f32 = jnp.float32

    force_ref[...] = jnp.zeros_like(force_ref)
    for load in loads[:8]:
        load.wait()
    meta_row = MIG * tiles * 9 - meta_at
    last = MIG * tiles * 8
    for c in range(9):
        moved_ref[c, 0:slots, :] = states_ref[c]
        for j in range(tiles):
            at = j * 16 + 2 * c if c < 8 else last + 2 * j
            moved_ref[c, slots:total, j * 128 : (j + 1) * 128] = jnp.concatenate(
                [beads_ref[d, at : at + MIG, :] for d in range(4)], axis=0
            )
    count = jnp.int32(0)
    blocks = bricks_ref.shape[1]
    row16 = lax.broadcasted_iota(jnp.int32, (total, 128), 0)
    active = jnp.zeros((total, 128), jnp.int32)
    for s in range(total):
        slot_ref[count] = s
        if s < slots:
            here = jnp.where(leave_ref[0, s] == 0, 1, 0)
        else:
            d, m = divmod(s - slots, MIG)
            here = jnp.where(meta_ref[d, meta_row + m, blocks] > 0.5, 1, 0)
        count = count + here
        active = jnp.where(row16 == s, here, active)

    rows = moved_ref[3:6].reshape(3 * total, vertices).astype(jnp.bfloat16)
    for g in range(quads):
        loads[8 + g].wait()
        part = jnp.dot(
            rows, stiff_ref[:, g * 256 : (g + 1) * 256], preferred_element_type=f32
        )
        node_ref[:, g * 256 : (g + 1) * 256] = -part

    loads[8 + parts].wait()
    sampled_ref[...] = jnp.zeros_like(sampled_ref)
    lane8 = lax.broadcasted_iota(jnp.int32, (8, 128), 1)
    row8 = lax.broadcasted_iota(jnp.int32, (8, 256), 0)
    steps8 = row8.astype(f32)
    group = lax.broadcasted_iota(jnp.int32, (8, 256), 1) // 64

    def couple(i, carry):
        s = slot_ref[i]
        own = s < slots
        inside = jnp.minimum(s, slots - 1)
        outside = jnp.maximum(s - slots, 0)
        for g in range(quads):
            cols = slice(g * 256, (g + 1) * 256)
            where = [
                jnp.where(
                    own,
                    bricks_ref[inside, 4 * g + j],
                    meta_ref[
                        outside // MIG, meta_row + outside % MIG, 4 * g + j
                    ].astype(jnp.int32),
                )
                for j in range(4)
            ]
            along_x = phi(moved_ref[0, pl.ds(s, 1), cols] - steps8)
            along_y = phi(moved_ref[1, pl.ds(s, 1), cols] - steps8)
            along_z = phi(moved_ref[2, pl.ds(s, 1), cols] - steps8)
            zx = [along_z[iz : iz + 1, :] * along_x for iz in range(8)]
            for k in range(4):
                for h in range(2):
                    iy = k + 4 * h
                    y_row = jnp.broadcast_to(along_y[iy : iy + 1, :], (8, 256))
                    for iz in range(0, 8, 2):
                        pair = jnp.concatenate([zx[iz] * y_row, zx[iz + 1] * y_row], axis=0)
                        at = (k * 2 + h) * 64 + iz * 8
                        weight_ref[g, at : at + 16, :] = pair.astype(jnp.bfloat16)
            near = jnp.concatenate([velocity_ref[r] for r in where], axis=0)
            flat = jnp.concatenate(zx, axis=0).astype(jnp.bfloat16)
            sampled = jnp.dot(
                near[:, 0:64].astype(jnp.bfloat16), flat, preferred_element_type=f32
            )
            for c in range(3):
                vertex = sampled[8 * c : 8 * c + 8, :]
                for j in range(1, 4):
                    at = 24 * j + 8 * c
                    vertex = jnp.where(group == j, sampled[at : at + 8, :], vertex)
                sampled_ref[c, pl.ds(s, 1), cols] = jnp.sum(
                    vertex * along_y, axis=0, keepdims=True
                )
            force = jnp.zeros((8, 256), f32)
            for c in range(3):
                force = jnp.where(row8 == c, node_ref[pl.ds(c * total + s, 1), cols], force)
            spreading = jnp.concatenate(
                [jnp.where(group == j, force, 0.0) for j in range(4)], axis=0
            ).astype(jnp.bfloat16)
            spread = lax.dot_general(
                spreading, weight_ref[g], (((1,), (1,)), ((), ())), preferred_element_type=f32
            )
            for j in range(4):
                for k in range(4):
                    force_ref[where[j], k] = (
                        force_ref[where[j], k]
                        + spread[8 * j : 8 * j + 8, k * 128 : (k + 1) * 128]
                    )
        return carry

    lax.fori_loop(0, count, couple, 0)

    for j in range(tiles):
        cols = slice(j * 128, (j + 1) * 128)
        for c in range(3):
            speed = sampled_ref[c, :, cols]
            half = 0.5 * (moved_ref[6 + c, :, cols] + speed)
            vertex_ref[c, :, cols] = jnp.where(active > 0, moved_ref[c, :, cols] + half, 0.0)
            vertex_ref[3 + c, :, cols] = jnp.where(
                active > 0, moved_ref[3 + c, :, cols] + half, 0.0
            )
            vertex_ref[6 + c, :, cols] = speed
    finished = pltpu.make_async_copy(vertex_ref, vertex_out, sems.at[depth])
    finished.start()

    for load in loads[9 + parts :]:
        load.wait()
    for axis in range(3):
        for bz in range(depth // 8):
            parts = []
            for by in range(by_count):
                laid = []
                for bx in range(bx_count):
                    brick = (bz * bx_count + bx) * by_count + by
                    got = [force_ref[brick, k, axis : axis + 1, :] for k in range(4)]
                    laid.append(jnp.concatenate(got + got, axis=0))
                top = lax.broadcasted_iota(jnp.int32, (8, 128), 0) < 4
                low = jnp.where(top, laid[0], pltpu.roll(laid[0], 64, 1))
                high = jnp.where(top, pltpu.roll(laid[1], 64, 1), laid[1])
                parts.append(jnp.where(lane8 < 64, low, high))
            cells = jnp.concatenate(parts, axis=0).T
            for bx in range(bx_count):
                for iz in range(8):
                    at = (bx * 8 + iz) * 8
                    field_ref[axis, bz * 8 + iz, bx * 8 : bx * 8 + 8, :] = cells[at : at + 8, :]

    def collide(z, carry):
        density, inverse = moment_ref[0, z], moment_ref[4, z]
        force = [field_ref[axis, z] for axis in range(3)]
        speed = [(moment_ref[1 + axis, z] + 0.5 * force[axis]) * inverse for axis in range(3)]
        square = speed[0] * speed[0] + speed[1] * speed[1] + speed[2] * speed[2]
        dot = speed[0] * force[0] + speed[1] * force[1] + speed[2] * force[2]
        fluid = solid_ref[z] == 0
        base = (1.25 * density) * (1.0 - 1.5 * square) - 1.125 * dot
        dense = 5.625 * density
        odd = [3.75 * density * speed[axis] + 1.125 * force[axis] for axis in range(3)]
        slope = [3.375 * force[axis] for axis in range(3)]
        rest = read_ref[0, z]
        fresh_ref[0, z] = jnp.where(fluid, WEIGHTS[0] * base - 0.25 * rest, rest)

        def along(vector, c):
            terms = None
            for axis in range(3):
                if c[axis] == 0:
                    continue
                if terms is None:
                    terms = vector[axis] if c[axis] == 1 else -vector[axis]
                else:
                    terms = terms + vector[axis] if c[axis] == 1 else terms - vector[axis]
            return terms

        for q in range(1, 19, 2):
            c = LATTICE[q]
            e = along(speed, c)
            even = WEIGHTS[q] * (base + e * (dense * e + along(slope, c)))
            skew = WEIGHTS[q] * along(odd, c)
            ahead, back = read_ref[q, z], read_ref[q + 1, z]
            fresh_ref[q, z] = jnp.where(fluid, even + skew - 0.25 * ahead, back)
            fresh_ref[q + 1, z] = jnp.where(fluid, even - skew - 0.25 * back, ahead)
        pltpu.make_async_copy(fresh_ref.at[:, z], pops_out.at[:, z], sems.at[z]).start()
        return carry

    lax.fori_loop(0, depth, collide, 0, unroll=2)

    def finish(z, carry):
        pltpu.make_async_copy(fresh_ref.at[:, z], pops_out.at[:, z], sems.at[z]).wait()
        return carry

    lax.fori_loop(0, depth, finish, 0)
    finished.wait()


def advance(leaving, bricks, states, beads, solid, read, moment, velocity, stiffness):
    depth, width = read.shape[1], read.shape[2]
    slots, vertices = states.shape[1], states.shape[2]
    total = slots + 4 * MIG
    n_bricks = velocity.shape[0]
    hbm = pl.BlockSpec(memory_space=pltpu.HBM)
    f32 = jnp.float32
    return pl.pallas_call(
        step_kernel,
        out_shape=(
            jax.ShapeDtypeStruct(read.shape, f32),
            jax.ShapeDtypeStruct((9, total, vertices), f32),
        ),
        in_specs=[hbm] * 9,
        out_specs=(hbm, hbm),
        scratch_shapes=[
            pltpu.SMEM(leaving.shape, jnp.int32),
            pltpu.SMEM(bricks.shape, jnp.int32),
            pltpu.SMEM((4, 8, 128), f32),
            pltpu.VMEM(states.shape, f32),
            pltpu.VMEM(beads.shape, f32),
            pltpu.VMEM(solid.shape, jnp.int32),
            pltpu.VMEM(read.shape, f32),
            pltpu.VMEM(moment.shape, f32),
            pltpu.VMEM(velocity.shape, f32),
            pltpu.VMEM(stiffness.shape, stiffness.dtype),
            pltpu.VMEM(read.shape, f32),
            pltpu.VMEM((3, depth, width, 128), f32),
            pltpu.VMEM((n_bricks, 4, 8, 128), f32),
            pltpu.VMEM((9, total, vertices), f32),
            pltpu.VMEM((total * 3, vertices), f32),
            pltpu.VMEM((3, total, vertices), f32),
            pltpu.VMEM((9, total, vertices), f32),
            pltpu.VMEM((vertices // 256, 512, 256), jnp.bfloat16),
            pltpu.SMEM((total + 1,), jnp.int32),
            pltpu.SemaphoreType.DMA((depth + 1,)),
            pltpu.SemaphoreType.DMA((12 + vertices // 256,)),
        ],
        compiler_params=pltpu.CompilerParams(vmem_limit_bytes=56 * 1024 * 1024),
        name="step",
    )(leaving, bricks, states, beads, solid, read, moment, velocity, stiffness)


def solution(mesh):
    sizes = (mesh.shape["gx"], mesh.shape["gy"])

    def local(populations, solid_mask, bead_states, bead_bricks, leave_dir, stiffness):
        states = bead_states.reshape(bead_states.shape[2:]).transpose(1, 0, 2)
        bricks = bead_bricks.reshape(bead_bricks.shape[2:])
        leaving = leave_dir.reshape((1,) + leave_dir.shape[2:])
        beads, read, moment, velocity = exchange(
            populations, states, bricks, leaving, sizes
        )
        populations_out, vertex_out = advance(
            leaving, bricks, states, beads, solid_mask, read, moment, velocity, stiffness
        )
        vertex_out = vertex_out.transpose(1, 0, 2)
        return (populations_out, vertex_out.reshape((1, 1) + vertex_out.shape))

    return jax.shard_map(
        local,
        mesh=mesh,
        in_specs=(
            P(None, None, "gx", "gy"),
            P(None, "gx", "gy"),
            P("gx", "gy", None, None, None),
            P("gx", "gy", None, None),
            P("gx", "gy", None),
            P(),
        ),
        out_specs=(P(None, None, "gx", "gy"), P("gx", "gy", None, None, None)),
        check_vma=False,
    )
```
